32 devices in a mesh: grp: 2 (over x), ch: 16 (over z, y, core).
Axes of the slice: x: 2, y: 2, z: 4, core: 2. Of those that a mesh axis runs over, the one named last changes fastest.
Arguments:
- features: bfloat16 [2048, 2048], P('ch', 'grp'), parts along dimension 1, may hold values from -50 to 50
- dw_weight: float32 [2048, 49], P('ch'), may hold values from -0.875 to 0.875
- norm_gain: float32 [2048], replicated, may hold values from 0.25 to 1.75
- layer_scale: float32 [2048], replicated, may hold values from 0.2 to 1
- w_in: bfloat16 [8192, 2048], P('ch'), may hold values from -0.125 to 0.125
- w_out: bfloat16 [8192, 2048], P('ch'), may hold values from -0.0625 to 0.0625
- w_head: bfloat16 [2048, 150], replicated, may hold values from -3 to 3
- labels: int32 [2048], P('grp'), parts along dimension 0, may hold values from 0 to 149
Outputs:
- d_features: float32 [2048, 2048], P('ch', 'grp'), parts along dimension 1
- d_dw: float32 [2048, 98], P('ch', 'grp'), parts along dimension 1
- d_scale: float32 [4096], P(('grp', 'ch')), parts along dimension 0
- d_w_in: float32 [16384, 2048], P(('grp', 'ch')), parts along dimension 0
- d_w_out: float32 [16384, 2048], P(('grp', 'ch')), parts along dimension 0
- d_head: float32 [2048, 300], P('ch', 'grp'), parts along dimension 1
- mean_loss: float32 [2], P('grp'), parts along dimension 0
The draws below stay inside these ranges and needn't reach their ends.
There are 2 independent parts, one for each index of `grp`. The reference program is written for one: setup_inputs(seed, part) draws one part's arguments, and reference() takes and returns one part's arrays. A program takes and returns all parts, laid end to end along the dimension named above; an argument that names none is the same for every part. Nothing has to cross between parts.
All inputs are finite; a program needn't handle non-finite values.
Results may differ from the reference program's by a relative error of at most 0.012.
Values may be sent and summed in bfloat16 or wider, within the bound.
A program may use at most 128 MiB of HBM per device.

```python
import math
import jax
import jax.numpy as jnp
from jax import lax

C = 2048
FF = 8192
K = 150
KS = 7
WIN_H = 32
WIN_W = 32
TOKENS = 1024


def draw_features(key, part):
    key_base, key_tok = jax.random.split(jax.random.fold_in(key, 11), 2)
    base = jnp.clip(jax.random.normal(key_base, (C, TOKENS), jnp.float32), -4.0, 4.0)
    ramp = 0.3 * jnp.power(10.0, jnp.arange(C, dtype=jnp.float32) / C)
    tok_scale = jnp.exp(jax.random.uniform(key_tok, (TOKENS,), jnp.float32, math.log(0.3), math.log(3.0)))
    values = base * ramp[:, None] * tok_scale[None, :]
    return jnp.clip(values, -50.0, 50.0).astype(jnp.bfloat16)


def draw_w_head(key, part):
    key_base = jax.random.fold_in(jax.random.fold_in(key, 23), 0)
    spread = 2.0 / math.sqrt(C)
    values = jnp.clip(jax.random.normal(key_base, (C, K), jnp.float32), -4.0, 4.0) * spread
    return jnp.clip(values, -3.0, 3.0).astype(jnp.bfloat16)


def plant(values, rng, least, largest):
    longest = values.shape.index(max(values.shape))
    spots = []
    for shift in (0, 1):
        where = [jax.random.randint(jax.random.fold_in(rng, axis), (), 0, length) for axis, length in enumerate(values.shape)]
        where[longest] = (where[longest] + shift) % values.shape[longest]
        spots.append(tuple(where))
    return values.at[spots[0]].set(least).at[spots[1]].set(largest)


def block_levels(stream_key, shape, cuts, least, top_value):
    loudness, own = 1.0, jax.random.fold_in(stream_key, 6)
    for position, parts in cuts:
        heights = jnp.exp(jax.random.uniform(jax.random.fold_in(own, position), (parts,), jnp.float32, least / len(cuts), top_value / len(cuts)))
        loudness = loudness * jnp.repeat(heights, shape[position] // parts).reshape([-1 if axis == position else 1 for axis in range(len(shape))])
    return loudness


def gaussian(key, extent, scale, most, cuts=(), kind=jnp.bfloat16):
    result = jax.random.normal(key, extent, jnp.float32) * scale
    if len(cuts) > 0:
        result = block_levels(key, extent, cuts, -0.22, 0.18) * result
    return jnp.clip(result, min=-most, max=most).astype(kind)


def setup_inputs(seed: int = 0, part: int = 0) -> dict:
    key_of = jax.random.split(jax.random.key(seed), 9)
    part_splits = jax.random.split(jax.random.fold_in(key_of[8], part), 9)
    features = draw_features(jax.random.fold_in(jax.random.fold_in(key_of[8], part), 71), part)
    dw_weight = gaussian(key_of[1], (C, KS * KS), (KS * KS) ** -0.5, 0.875, ((0, 16),), jnp.float32)
    norm_gain = jnp.clip(1.0 + 0.15 * jax.random.normal(key_of[2], (C,), jnp.float32), 0.25, 1.75)
    layer_scale = jnp.clip(jnp.exp(jax.random.uniform(key_of[3], (C,), jnp.float32, math.log(0.2), math.log(1.0))), 0.2, 1.0)
    w_in = gaussian(key_of[4], (FF, C), C ** -0.5, 0.125, ((0, 16),))
    w_out = gaussian(key_of[5], (FF, C), FF ** -0.5, 0.0625, ((0, 16),))
    w_head = draw_w_head(jax.random.fold_in(key_of[8], 71), part)
    labels = plant(jax.random.randint(part_splits[7], (TOKENS,), 0, K), jax.random.fold_in(part_splits[7], 1), 0, K - 1).astype(jnp.int32)
    return {"features": features, "dw_weight": dw_weight, "norm_gain": norm_gain, "layer_scale": layer_scale, "w_in": w_in, "w_out": w_out, "w_head": w_head, "labels": labels}


norm_eps = 1e-06

def conv_apply(in_grid, kernel):
    half = KS // 2
    padded = jnp.pad(in_grid, ((0, 0), (half, half), (half, half)))
    running = jnp.zeros(in_grid.shape, in_grid.dtype)
    for row_shift in range(KS):
        for col_shift in range(KS):
            tap = kernel[:, row_shift * KS + col_shift]
            running = running + tap[:, None, None] * padded[:, row_shift:row_shift + WIN_H, col_shift:col_shift + WIN_W]
    return running

def gelu_parts(values):
    cum_prob = 0.5 * (1.0 + lax.erf(values * 0.7071067811865476))
    density = jnp.exp(-0.5 * values * values) * 0.3989422804014327
    return (values * cum_prob, cum_prob + values * density)

def reference(features, dw_weight, norm_gain, layer_scale, w_in, w_out, w_head, labels):
    highest = lax.Precision.HIGHEST
    inputs_wide = features.astype(jnp.float32)
    in_grid = inputs_wide.reshape(C, WIN_H, WIN_W)
    conv_out = conv_apply(in_grid, dw_weight).reshape(C, TOKENS).astype(jnp.bfloat16)
    conv_wide = conv_out.astype(jnp.float32)
    tok_mean = lax.optimization_barrier(jnp.mean(conv_wide, axis=0))
    centered = conv_wide - tok_mean[None, :]
    tok_var = lax.optimization_barrier(jnp.mean(centered * centered, axis=0))
    inv_std = 1.0 / jnp.sqrt(tok_var + norm_eps)
    normed = centered * inv_std[None, :]
    norm_out = (norm_gain[:, None] * normed).astype(jnp.bfloat16)
    pre_act = jnp.dot(w_in, norm_out, preferred_element_type=jnp.float32)
    gelu_out, gelu_slope = gelu_parts(pre_act)
    hidden = gelu_out.astype(jnp.bfloat16)
    branch_sum = lax.dot_general(w_out, hidden, (((0,), (0,)), ((), ())), preferred_element_type=jnp.float32)
    block_out = inputs_wide + layer_scale[:, None] * branch_sum
    head_wide = w_head.astype(jnp.float32)
    logits = lax.dot_general(block_out, head_wide, (((0,), (0,)), ((), ())), precision=highest)
    row_max = lax.optimization_barrier(jnp.max(logits, axis=1, keepdims=True))
    exp_terms = jnp.exp(logits - row_max)
    exp_total = lax.optimization_barrier(jnp.sum(exp_terms, axis=1, keepdims=True))
    log_total = jnp.log(exp_total) + row_max
    onehot = (labels[:, None] == jnp.arange(K, dtype=jnp.int32)[None, :]).astype(jnp.float32)
    picked = lax.optimization_barrier(jnp.sum(logits * onehot, axis=1))
    mean_loss = jnp.mean(log_total[:, 0] - picked).reshape(1)
    logit_grad = exp_terms / exp_total - onehot
    out_grad = lax.dot_general(head_wide, logit_grad, (((1,), (1,)), ((), ())), precision=highest)
    d_head = jnp.dot(block_out, logit_grad, precision=highest)
    d_scale = lax.optimization_barrier(jnp.sum(out_grad * branch_sum, axis=1))
    branch_grad = (layer_scale[:, None] * out_grad).astype(jnp.bfloat16)
    hidden_grad = jnp.dot(w_out, branch_grad, preferred_element_type=jnp.float32)
    d_w_out = lax.dot_general(hidden, branch_grad, (((1,), (1,)), ((), ())), preferred_element_type=jnp.float32)
    pre_grad = (hidden_grad * gelu_slope).astype(jnp.bfloat16)
    d_w_in = lax.dot_general(pre_grad, norm_out, (((1,), (1,)), ((), ())), preferred_element_type=jnp.float32)
    norm_grad = lax.dot_general(w_in, pre_grad, (((0,), (0,)), ((), ())), preferred_element_type=jnp.float32)
    gained = norm_gain[:, None] * norm_grad
    conv_grad = (gained - lax.optimization_barrier(jnp.mean(gained, axis=0))[None, :] - normed * lax.optimization_barrier(jnp.mean(gained * normed, axis=0))[None, :]) * inv_std[None, :]
    unused, pullback = jax.vjp(conv_apply, in_grid, dw_weight)
    grid_grad, d_dw = pullback(conv_grad.reshape(C, WIN_H, WIN_W))
    d_features = out_grad + grid_grad.reshape(C, TOKENS)
    return (d_features, d_dw, d_scale, d_w_in, d_w_out, d_head, mean_loss)
```

```python
import functools
import jax
import jax.numpy as jnp
from jax import lax
from jax.experimental import pallas as pl
from jax.experimental.pallas import tpu as pltpu
from jax.sharding import PartitionSpec as P

KS = 7
WIN_H = 32
WIN_W = 32

norm_eps = 1e-06
VMEM_LIMIT = 56 * 1024 * 1024


def conv_apply(in_grid, kernel):
    half = KS // 2
    padded = jnp.pad(in_grid, ((0, 0), (half, half), (half, half)))
    running = jnp.zeros(in_grid.shape, in_grid.dtype)
    for row_shift in range(KS):
        for col_shift in range(KS):
            tap = kernel[:, row_shift * KS + col_shift]
            running = (
                running
                + tap[:, None, None]
                * padded[:, row_shift : row_shift + WIN_H, col_shift : col_shift + WIN_W]
            )
    return running


def gelu_parts(values):
    cum_prob = 0.5 * (1.0 + lax.erf(values * 0.7071067811865476))
    density = jnp.exp(-0.5 * values * values) * 0.3989422804014327
    return (values * cum_prob, cum_prob + values * density)


def place(n):
    me = lax.axis_index("ch")
    return lax.div(me, 4), lax.rem(lax.div(me, 2), 2), lax.rem(me, 2)


def index_of(z, y, c):
    return (z * 2 + y) * 2 + c


def greet(devices, z, a):
    barrier = pltpu.get_barrier_semaphore()
    for device in devices:
        pl.semaphore_signal(barrier, inc=1, device_id={"ch": device})
    me = lax.axis_index("ch")

    @pl.when(z > 0)
    def _():
        pl.semaphore_signal(barrier, inc=1, device_id={"ch": me - 4})

    @pl.when(z < a - 1)
    def _():
        pl.semaphore_signal(barrier, inc=1, device_id={"ch": me + 4})

    count = len(devices) + jnp.where(z > 0, 1, 0) + jnp.where(z < a - 1, 1, 0)
    pl.semaphore_wait(barrier, count)


def gather_kernel(n, x_ref, out_ref, send_sem, recv_sem):
    a = n // 4
    rows = x_ref.shape[0]
    z, y, c = place(n)
    me = index_of(z, y, c)
    twin, across = index_of(z, y, 1 - c), index_of(z, 1 - y, c)
    greet([twin, across], z, a)

    def block(b):
        return out_ref.at[pl.ds(pl.multiple_of(b * rows, rows), rows)]

    def copy(kind, b, device):
        return pltpu.make_async_remote_copy(
            src_ref=block(b),
            dst_ref=block(b),
            send_sem=send_sem.at[kind, b],
            recv_sem=recv_sem.at[b],
            device_id={"ch": device},
        )

    out_ref[pl.ds(pl.multiple_of(me * rows, rows), rows)] = x_ref[...]

    @pl.when(z < a - 1)
    def _():
        copy(0, me, me + 4).start()

    @pl.when(z > 0)
    def _():
        copy(1, me, me - 4).start()

    copy(2, me, across).start()
    copy(3, me, twin).start()

    def from_line(s):
        below, above = me - 4 * s, me + 4 * s

        @pl.when(z >= s)
        def _():
            copy(0, below, me).wait_recv()

            @pl.when(z < a - 1)
            def _():
                copy(0, below, me + 4).start()

            copy(2, below, across).start()
            copy(3, below, twin).start()

        @pl.when(z + s < a)
        def _():
            copy(1, above, me).wait_recv()

            @pl.when(z > 0)
            def _():
                copy(1, above, me - 4).start()

            copy(2, above, across).start()
            copy(3, above, twin).start()

    def from_across(s):
        def take(b):
            copy(2, b, across).wait_recv()
            copy(3, b, twin).start()

        if s == 0:
            take(across)
            return

        @pl.when(z >= s)
        def _():
            take(across - 4 * s)

        @pl.when(z + s < a)
        def _():
            take(across + 4 * s)

    for s in range(1, a):
        from_line(s)
        from_across(s - 1)
    from_across(a - 1)

    for q in range(n // 2):
        copy(3, q * 2 + 1 - c, twin).wait_recv()
        copy(3, q * 2 + c, twin).wait_send()
    for zz in range(a):
        copy(2, index_of(zz, y, c), across).wait_send()

        @pl.when((z < a - 1) & (zz <= z))
        def _():
            copy(0, index_of(zz, y, c), me + 4).wait_send()

        @pl.when((z > 0) & (zz >= z))
        def _():
            copy(1, index_of(zz, y, c), me - 4).wait_send()


def gather(n, x):
    rows, cols = x.shape
    return pl.pallas_call(
        functools.partial(gather_kernel, n),
        out_shape=jax.ShapeDtypeStruct((n * rows, cols), x.dtype),
        in_specs=[pl.BlockSpec(memory_space=pltpu.VMEM)],
        out_specs=pl.BlockSpec(memory_space=pltpu.VMEM),
        scratch_shapes=[pltpu.SemaphoreType.DMA((4, n)), pltpu.SemaphoreType.DMA((n,))],
        compiler_params=pltpu.CompilerParams(
            collective_id=0, has_side_effects=True, vmem_limit_bytes=VMEM_LIMIT
        ),
    )(x)


def total_kernel(n, x_ref, out_ref, buf, from_twin, acc, slots, sums, t_sem, r_sem, g_sem, f_sem):
    m = n // 2
    height, cols = x_ref.shape
    strips = cols // 128
    half = height * strips // 2
    rows = half // m
    me = lax.axis_index("ch")
    q, c = lax.div(me, 2), lax.rem(me, 2)
    twin = q * 2 + 1 - c
    barrier = pltpu.get_barrier_semaphore()
    pl.semaphore_signal(barrier, inc=1, device_id={"ch": twin})
    for d in range(1, m):
        pl.semaphore_signal(barrier, inc=1, device_id={"ch": lax.rem(q + d, m) * 2 + c})
    for j in range(strips):
        buf[j * height : (j + 1) * height, :] = x_ref[:, j * 128 : (j + 1) * 128]
    pl.semaphore_wait(barrier, m)

    def piece(ref, start, length):
        return ref.at[pl.ds(pl.multiple_of(start, 8), length)]

    swap = pltpu.make_async_remote_copy(
        src_ref=piece(buf, (1 - c) * half, half),
        dst_ref=from_twin,
        send_sem=t_sem.at[0],
        recv_sem=t_sem.at[1],
        device_id={"ch": twin},
    )
    swap.start()
    swap.wait_recv()
    acc[...] = buf[pl.ds(pl.multiple_of(c * half, 8), half), :] + from_twin[...]

    def scatter(d):
        other = lax.rem(q + d, m)
        return pltpu.make_async_remote_copy(
            src_ref=piece(acc, other * rows, rows),
            dst_ref=slots.at[d],
            send_sem=r_sem.at[0, d],
            recv_sem=r_sem.at[1, d],
            device_id={"ch": other * 2 + c},
        )

    for d in range(1, m):
        scatter(d).start()
    mine = acc[pl.ds(pl.multiple_of(q * rows, 8), rows), :]
    for d in range(1, m):
        scatter(d).wait_recv()
        mine = mine + slots[d]
    my_start = c * half + q * rows
    sums[pl.ds(pl.multiple_of(my_start, 8), rows), :] = mine

    def spread(d, start, device):
        return pltpu.make_async_remote_copy(
            src_ref=piece(sums, start, rows),
            dst_ref=piece(sums, start, rows),
            send_sem=g_sem.at[0, d],
            recv_sem=g_sem.at[1, d],
            device_id={"ch": device},
        )

    def forward(d, start):
        return pltpu.make_async_remote_copy(
            src_ref=piece(sums, start, rows),
            dst_ref=piece(sums, start, rows),
            send_sem=f_sem.at[0, d],
            recv_sem=f_sem.at[1, d],
            device_id={"ch": twin},
        )

    for d in range(1, m):
        spread(d, my_start, lax.rem(q + d, m) * 2 + c).start()
    forward(0, my_start).start()
    for d in range(1, m):
        start = c * half + lax.rem(q - d + m, m) * rows
        spread(d, start, twin).wait_recv()
        forward(d, start).start()
    for d in range(m):
        forward(d, (1 - c) * half + lax.rem(q - d + m, m) * rows).wait_recv()
    for j in range(strips):
        out_ref[:, j * 128 : (j + 1) * 128] = sums[j * height : (j + 1) * height, :]
    swap.wait_send()
    for d in range(1, m):
        scatter(d).wait_send()
        spread(d, my_start, twin).wait_send()
    for d in range(m):
        forward(d, my_start).wait_send()


def total(n, x):
    height, cols = x.shape
    area = height * (cols // 128)
    m = n // 2
    return pl.pallas_call(
        functools.partial(total_kernel, n),
        out_shape=jax.ShapeDtypeStruct(x.shape, x.dtype),
        in_specs=[pl.BlockSpec(memory_space=pltpu.VMEM)],
        out_specs=pl.BlockSpec(memory_space=pltpu.VMEM),
        scratch_shapes=[
            pltpu.VMEM((area, 128), jnp.float32),
            pltpu.VMEM((area // 2, 128), jnp.float32),
            pltpu.VMEM((area // 2, 128), jnp.float32),
            pltpu.VMEM((m, area // n, 128), jnp.float32),
            pltpu.VMEM((area, 128), jnp.float32),
            pltpu.SemaphoreType.DMA((2,)),
            pltpu.SemaphoreType.DMA((2, m)),
            pltpu.SemaphoreType.DMA((2, m)),
            pltpu.SemaphoreType.DMA((2, m)),
        ],
        compiler_params=pltpu.CompilerParams(
            collective_id=1, has_side_effects=True, vmem_limit_bytes=VMEM_LIMIT
        ),
    )(x)


def scatter_kernel(
    n, g_ref, out_ref, t_in, y_in, u_in, d_in, y_out, z_out, t_sem, y_sem, u_sem, d_sem, zs_sem
):
    a = n // 4
    rows = out_ref.shape[0]
    z, y, c = place(n)
    me = index_of(z, y, c)
    twin, across = index_of(z, y, 1 - c), index_of(z, 1 - y, c)
    greet([twin, across], z, a)

    def own(b):
        return pl.ds(pl.multiple_of(b * rows, rows), rows)

    def order(k):
        if k == a - 1:
            return z
        low = jnp.where(k < a - 1 - z, a - 1 - k, k - (a - 1 - z))
        high = jnp.where(k < z, k, a - 1 - (k - z))
        return jnp.where(2 * z < a, low, high)

    def to_twin(zz, side, core):
        return pltpu.make_async_remote_copy(
            src_ref=g_ref.at[own(index_of(zz, side, core))],
            dst_ref=t_in.at[zz * 2 + side],
            send_sem=t_sem.at[0, zz * 2 + side],
            recv_sem=t_sem.at[1, zz * 2 + side],
            device_id={"ch": twin},
        )

    def to_across(k, zz):
        return pltpu.make_async_remote_copy(
            src_ref=y_out.at[k],
            dst_ref=y_in.at[zz],
            send_sem=y_sem.at[0, zz],
            recv_sem=y_sem.at[1, zz],
            device_id={"ch": across},
        )

    def along(k, zz, landing, sem, device):
        return pltpu.make_async_remote_copy(
            src_ref=z_out.at[k],
            dst_ref=landing.at[zz],
            send_sem=zs_sem.at[k],
            recv_sem=sem.at[zz],
            device_id={"ch": device},
        )

    for k in range(a):
        to_twin(order(k), 1 - y, 1 - c).start()
    for k in range(a):
        to_twin(order(k), y, 1 - c).start()
    for k in range(a):
        zz = order(k)
        to_twin(zz, 1 - y, c).wait_recv()
        y_out[k] = (
            g_ref[own(index_of(zz, 1 - y, c))].astype(jnp.float32)
            + t_in[zz * 2 + 1 - y].astype(jnp.float32)
        ).astype(jnp.bfloat16)
        to_across(k, zz).start()
    for k in range(a):
        zz = order(k)
        to_twin(zz, y, c).wait_recv()
        to_across(k, zz).wait_recv()
        term = (
            g_ref[own(index_of(zz, y, c))].astype(jnp.float32)
            + t_in[zz * 2 + y].astype(jnp.float32)
            + y_in[zz].astype(jnp.float32)
        )
        if k < a - 1:
            out_ref[...] = term

            @pl.when((zz > z) & (z > 0))
            def _():
                along(k, zz, u_in, u_sem, me).wait_recv()
                out_ref[...] += u_in[zz].astype(jnp.float32)

            @pl.when((zz < z) & (z < a - 1))
            def _():
                along(k, zz, d_in, d_sem, me).wait_recv()
                out_ref[...] += d_in[zz].astype(jnp.float32)

            z_out[k] = out_ref[...].astype(jnp.bfloat16)

            @pl.when(zz > z)
            def _():
                along(k, zz, u_in, u_sem, me + 4).start()

            @pl.when(zz < z)
            def _():
                along(k, zz, d_in, d_sem, me - 4).start()

        else:
            out_ref[...] = term

            @pl.when(z > 0)
            def _():
                along(0, z, u_in, u_sem, me).wait_recv()
                out_ref[...] += u_in[z].astype(jnp.float32)

            @pl.when(z < a - 1)
            def _():
                along(0, z, d_in, d_sem, me).wait_recv()
                out_ref[...] += d_in[z].astype(jnp.float32)

    for k in range(a):
        zz = order(k)
        to_twin(zz, 1 - y, 1 - c).wait_send()
        to_twin(zz, y, 1 - c).wait_send()
        to_across(k, zz).wait_send()
        if k < a - 1:
            along(k, zz, u_in, u_sem, me).wait_send()


def scatter(n, g):
    rows, cols = g.shape[0] // n, g.shape[1]
    a = n // 4
    return pl.pallas_call(
        functools.partial(scatter_kernel, n),
        out_shape=jax.ShapeDtypeStruct((rows, cols), jnp.float32),
        in_specs=[pl.BlockSpec(memory_space=pltpu.VMEM)],
        out_specs=pl.BlockSpec(memory_space=pltpu.VMEM),
        scratch_shapes=[
            pltpu.VMEM((n // 2, rows, cols), jnp.bfloat16),
            pltpu.VMEM((a, rows, cols), jnp.bfloat16),
            pltpu.VMEM((a, rows, cols), jnp.bfloat16),
            pltpu.VMEM((a, rows, cols), jnp.bfloat16),
            pltpu.VMEM((a, rows, cols), jnp.bfloat16),
            pltpu.VMEM((a, rows, cols), jnp.bfloat16),
            pltpu.SemaphoreType.DMA((2, n // 2)),
            pltpu.SemaphoreType.DMA((2, a)),
            pltpu.SemaphoreType.DMA((a,)),
            pltpu.SemaphoreType.DMA((a,)),
            pltpu.SemaphoreType.DMA((a,)),
        ],
        compiler_params=pltpu.CompilerParams(
            collective_id=2, has_side_effects=True, vmem_limit_bytes=VMEM_LIMIT
        ),
    )(g)


def dot(lhs, rhs, over, precision=None):
    return lax.dot_general(
        lhs, rhs, ((over[:1], over[1:]), ((), ())),
        precision=precision, preferred_element_type=jnp.float32,
    )


def per_device(n, features, dw_weight, norm_gain, layer_scale, w_in, w_out, w_head, labels):
    fine = lax.Precision.HIGH
    my_rows, tok_count = features.shape
    channels, class_count = w_head.shape
    row_offset = lax.axis_index("ch") * my_rows
    inputs_wide = features.astype(jnp.float32)
    in_grid = inputs_wide.reshape(my_rows, WIN_H, WIN_W)
    conv_out = conv_apply(in_grid, dw_weight).reshape(my_rows, tok_count).astype(jnp.bfloat16)
    conv_all = gather(n, conv_out)
    conv_wide = conv_all.astype(jnp.float32)
    tok_mean = jnp.mean(conv_wide, axis=0)
    centered = conv_wide - tok_mean[None, :]
    tok_var = jnp.mean(centered * centered, axis=0)
    inv_std = 1.0 / jnp.sqrt(tok_var + norm_eps)
    norm_out = (norm_gain[:, None] * (centered * inv_std[None, :])).astype(jnp.bfloat16)
    pre_act = jnp.dot(w_in, norm_out, preferred_element_type=jnp.float32)
    gelu_out, gelu_slope = gelu_parts(pre_act)
    hidden = gelu_out.astype(jnp.bfloat16)

    classes = -(-class_count // max(n, 16)) * max(n, 16)
    head_pad = jnp.pad(w_head, ((0, 0), (0, classes - class_count)))
    head_wide = head_pad.astype(jnp.float32)
    my_scale = lax.dynamic_slice_in_dim(layer_scale, row_offset, my_rows, 0)
    my_head = lax.dynamic_slice_in_dim(head_pad, row_offset, my_rows, 0)
    my_head_wide = my_head.astype(jnp.float32)
    scaled_head = layer_scale[:, None] * head_wide
    mixed = dot(w_out.astype(jnp.float32), scaled_head, (1, 0), fine)
    part = dot(mixed, hidden.astype(jnp.float32), (0, 0), fine) + dot(my_head, features, (0, 0))
    logits = total(n, part)

    kinds = lax.broadcasted_iota(jnp.int32, (classes, tok_count), 0)
    logits = jnp.where(kinds < class_count, logits, -jnp.inf)
    row_max = jnp.max(logits, axis=0, keepdims=True)
    exp_terms = jnp.exp(logits - row_max)
    exp_total = jnp.sum(exp_terms, axis=0, keepdims=True)
    log_total = jnp.log(exp_total) + row_max
    hit = kinds == labels[None, :]
    picked = jnp.sum(jnp.where(hit, logits, 0.0), axis=0)
    mean_loss = jnp.mean(log_total[0] - picked).reshape(1)
    logit_grad = exp_terms / exp_total - hit.astype(jnp.float32)
    grad_narrow = logit_grad.astype(jnp.bfloat16)

    out_grad = dot(my_head_wide, logit_grad, (1, 0), fine)
    seen = dot(hidden, grad_narrow, (1, 1))
    hidden_grad = dot(mixed, logit_grad, (1, 0), fine)
    seen_narrow = seen.astype(jnp.bfloat16)
    d_w_out = dot(seen_narrow, scaled_head.astype(jnp.bfloat16), (1, 1))
    branch_seen = dot(w_out, seen_narrow, (0, 0)).astype(jnp.bfloat16)
    pre_grad_wide = hidden_grad * gelu_slope
    pre_grad = pre_grad_wide.astype(jnp.bfloat16)
    d_w_in = dot(pre_grad, norm_out, (1, 1))
    gain_rows = jnp.sum(w_in.astype(jnp.float32) * norm_gain[None, :], axis=1)
    mean_gained = jnp.sum(gain_rows[:, None] * pre_grad_wide, axis=0) / channels
    mean_both = jnp.sum(pre_act * pre_grad_wide, axis=0) / channels
    norm_grad = dot(w_in, pre_grad, (0, 0))
    conv_term = (
        norm_gain[:, None] * norm_grad
        - mean_gained[None, :]
        - (centered * inv_std[None, :]) * mean_both[None, :]
    ) * inv_std[None, :]
    width = -(-classes // 128) * 128
    payload = jnp.concatenate(
        [
            conv_term.astype(jnp.bfloat16),
            jnp.pad(branch_seen, ((0, 0), (0, width - classes))),
        ],
        axis=1,
    )
    landed = scatter(n, payload)
    conv_grad = landed[:, :tok_count]
    my_seen = landed[:, tok_count : tok_count + class_count]
    d_head = dot(inputs_wide, logit_grad, (1, 1), fine)[:, :class_count] + my_scale[:, None] * my_seen
    d_scale = jnp.sum(my_head_wide[:, :class_count] * my_seen, axis=1)
    unused, pullback = jax.vjp(conv_apply, in_grid, dw_weight)
    grid_grad, d_dw = pullback(conv_grad.reshape(my_rows, WIN_H, WIN_W))
    d_features = out_grad + grid_grad.reshape(my_rows, tok_count)
    return (d_features, d_dw, d_scale, d_w_in, d_w_out, d_head, mean_loss)


def solution(mesh):
    placed = (P("ch", "grp"), P("ch", None), P(), P(), P("ch", None), P("ch", None), P(), P("grp"))
    return jax.shard_map(
        functools.partial(per_device, mesh.shape["ch"]),
        mesh=mesh,
        in_specs=placed,
        out_specs=(
            P("ch", "grp"),
            P("ch", "grp"),
            P(("grp", "ch")),
            P(("grp", "ch"), None),
            P(("grp", "ch"), None),
            P("ch", "grp"),
            P("grp"),
        ),
        check_vma=False,
    )
```

```python
import functools
import jax
import jax.numpy as jnp
from jax import lax
from jax.experimental import pallas as pl
from jax.experimental.pallas import tpu as pltpu
from jax.sharding import PartitionSpec as P

KS = 7
WIN_H = 32
WIN_W = 32

norm_eps = 1e-06
VMEM_LIMIT = 56 * 1024 * 1024


def slide(values, rows, cols):
    area = values.shape[1]
    token = lax.broadcasted_iota(jnp.int32, values.shape, 1)
    step = rows * WIN_W + cols
    if step == 0:
        return values
    if cols:
        spot = lax.rem(token, WIN_W) + cols
        inside = (spot >= 0) & (spot < WIN_W)
    else:
        spot = token + step
        inside = (spot >= 0) & (spot < area)
    return jnp.where(inside, pltpu.roll(values, (-step) % area, 1), 0.0)


def conv_rows(values, taps):
    half = KS // 2
    shifted = [slide(values, 0, j - half) for j in range(KS)]
    running = None
    for i in range(KS):
        line = sum(taps[:, i * KS + j : i * KS + j + 1] * shifted[j] for j in range(KS))
        line = slide(line, i - half, 0)
        running = line if running is None else running + line
    return running


def conv_back_kernel(grad_ref, x_ref, taps_ref, add_ref, dx_ref, dtaps_ref):
    half = KS // 2
    wide = dtaps_ref.shape[1]

    @pl.loop(0, x_ref.shape[0] // 8)
    def _(g):
        own = pl.ds(pl.multiple_of(g * 8, 8), 8)
        grad, values, taps = grad_ref[own, :], x_ref[own, :], taps_ref[own, :]
        lifted = [slide(grad, half - i, 0) for i in range(KS)]
        column = lax.broadcasted_iota(jnp.int32, (8, wide), 1)
        dtaps = jnp.zeros((8, wide), jnp.float32)
        dx = add_ref[own, :]
        for j in range(KS):
            line = sum(taps[:, i * KS + j : i * KS + j + 1] * lifted[i] for i in range(KS))
            dx = dx + slide(line, 0, half - j)
            shifted = slide(values, 0, j - half)
            for i in range(KS):
                whole = jnp.sum(lifted[i] * shifted, axis=1, keepdims=True)
                dtaps = jnp.where(column == i * KS + j, whole, dtaps)
        dx_ref[own, :] = dx
        dtaps_ref[own, :] = dtaps


def conv_back(grad, values, taps, add):
    return pl.pallas_call(
        conv_back_kernel,
        out_shape=(
            jax.ShapeDtypeStruct(grad.shape, jnp.float32),
            jax.ShapeDtypeStruct(taps.shape, jnp.float32),
        ),
        in_specs=[pl.BlockSpec(memory_space=pltpu.VMEM)] * 4,
        out_specs=(pl.BlockSpec(memory_space=pltpu.VMEM),) * 2,
        compiler_params=pltpu.CompilerParams(vmem_limit_bytes=32 * 1024 * 1024),
    )(grad, values, taps, add)


def gelu_parts(values):
    cum_prob = 0.5 * (1.0 + lax.erf(values * 0.7071067811865476))
    density = jnp.exp(-0.5 * values * values) * 0.3989422804014327
    return (values * cum_prob, cum_prob + values * density)


def place(n):
    me = lax.axis_index("ch")
    return lax.div(me, 4), lax.rem(lax.div(me, 2), 2), lax.rem(me, 2)


def index_of(z, y, c):
    return (z * 2 + y) * 2 + c


def greet(devices, z, a, between=None):
    barrier = pltpu.get_barrier_semaphore()
    for device in devices:
        pl.semaphore_signal(barrier, inc=1, device_id={"ch": device})
    me = lax.axis_index("ch")

    @pl.when(z > 0)
    def _():
        pl.semaphore_signal(barrier, inc=1, device_id={"ch": me - 4})

    @pl.when(z < a - 1)
    def _():
        pl.semaphore_signal(barrier, inc=1, device_id={"ch": me + 4})

    if between is not None:
        between()
    count = len(devices) + jnp.where(z > 0, 1, 0) + jnp.where(z < a - 1, 1, 0)
    pl.semaphore_wait(barrier, count)


def gather_kernel(
    n, x_ref, taps_ref, w_ref, head_ref, out_ref, mixed_ref, wide, conv, send_sem, recv_sem
):
    a = n // 4
    rows = x_ref.shape[0]
    z, y, c = place(n)
    me = index_of(z, y, c)
    twin, across = index_of(z, y, 1 - c), index_of(z, 1 - y, c)

    def convolve():
        wide[...] = x_ref[...].astype(jnp.float32)

        @pl.loop(0, rows // 8)
        def _(g):
            own = pl.ds(pl.multiple_of(g * 8, 8), 8)
            conv[own, :] = conv_rows(wide[own, :], taps_ref[own, :])

        out_ref[pl.ds(pl.multiple_of(me * rows, rows), rows)] = conv[...].astype(jnp.bfloat16)

    greet([twin, across], z, a, convolve)

    def block(b):
        return out_ref.at[pl.ds(pl.multiple_of(b * rows, rows), rows)]

    def copy(kind, b, device):
        return pltpu.make_async_remote_copy(
            src_ref=block(b),
            dst_ref=block(b),
            send_sem=send_sem.at[kind, b],
            recv_sem=recv_sem.at[b],
            device_id={"ch": device},
        )

    @pl.when(z < a - 1)
    def _():
        copy(0, me, me + 4).start()

    @pl.when(z > 0)
    def _():
        copy(1, me, me - 4).start()

    copy(2, me, across).start()
    copy(3, me, twin).start()

    head = head_ref[...]
    high = head.astype(jnp.bfloat16)
    low = (head - high.astype(jnp.float32)).astype(jnp.bfloat16)
    units = w_ref.shape[0]
    part = min(units, 128)

    @pl.loop(0, units // part)
    def _(g):
        own = pl.ds(pl.multiple_of(g * part, part), part)
        weights = w_ref[own, :]
        mixed_ref[own, :] = jnp.dot(
            weights, high, preferred_element_type=jnp.float32
        ) + jnp.dot(weights, low, preferred_element_type=jnp.float32)

    def from_line(s):
        below, above = me - 4 * s, me + 4 * s

        @pl.when(z >= s)
        def _():
            copy(0, below, me).wait_recv()

            @pl.when(z < a - 1)
            def _():
                copy(0, below, me + 4).start()

            copy(2, below, across).start()
            copy(3, below, twin).start()

        @pl.when(z + s < a)
        def _():
            copy(1, above, me).wait_recv()

            @pl.when(z > 0)
            def _():
                copy(1, above, me - 4).start()

            copy(2, above, across).start()
            copy(3, above, twin).start()

    def from_across(s):
        def take(b):
            copy(2, b, across).wait_recv()
            copy(3, b, twin).start()

        if s == 0:
            take(across)
            return

        @pl.when(z >= s)
        def _():
            take(across - 4 * s)

        @pl.when(z + s < a)
        def _():
            take(across + 4 * s)

    for s in range(1, a):
        from_line(s)
        from_across(s - 1)
    from_across(a - 1)

    for q in range(n // 2):
        copy(3, q * 2 + 1 - c, twin).wait_recv()
        copy(3, q * 2 + c, twin).wait_send()
    for zz in range(a):
        copy(2, index_of(zz, y, c), across).wait_send()

        @pl.when((z < a - 1) & (zz <= z))
        def _():
            copy(0, index_of(zz, y, c), me + 4).wait_send()

        @pl.when((z > 0) & (zz >= z))
        def _():
            copy(1, index_of(zz, y, c), me - 4).wait_send()


def gather(n, x, taps, weights, head):
    rows, cols = x.shape
    return pl.pallas_call(
        functools.partial(gather_kernel, n),
        out_shape=(
            jax.ShapeDtypeStruct((n * rows, cols), x.dtype),
            jax.ShapeDtypeStruct((weights.shape[0], head.shape[1]), jnp.float32),
        ),
        in_specs=[pl.BlockSpec(memory_space=pltpu.VMEM)] * 4,
        out_specs=(pl.BlockSpec(memory_space=pltpu.VMEM),) * 2,
        scratch_shapes=[
            pltpu.VMEM((rows, cols), jnp.float32),
            pltpu.VMEM((rows, cols), jnp.float32),
            pltpu.SemaphoreType.DMA((4, n)),
            pltpu.SemaphoreType.DMA((n,)),
        ],
        compiler_params=pltpu.CompilerParams(
            collective_id=0, has_side_effects=True, vmem_limit_bytes=VMEM_LIMIT
        ),
    )(x, taps, weights, head)


def total_kernel(n, x_ref, out_ref, buf, from_twin, acc, slots, sums, t_sem, r_sem, g_sem, f_sem):
    m = n // 2
    height, cols = x_ref.shape
    strips = cols // 128
    half = height * strips // 2
    rows = half // m
    me = lax.axis_index("ch")
    q, c = lax.div(me, 2), lax.rem(me, 2)
    twin = q * 2 + 1 - c
    barrier = pltpu.get_barrier_semaphore()
    pl.semaphore_signal(barrier, inc=1, device_id={"ch": twin})
    for d in range(1, m):
        pl.semaphore_signal(barrier, inc=1, device_id={"ch": lax.rem(q + d, m) * 2 + c})
    for j in range(strips):
        buf[j * height : (j + 1) * height, :] = x_ref[:, j * 128 : (j + 1) * 128]
    pl.semaphore_wait(barrier, m)

    def piece(ref, start, length):
        return ref.at[pl.ds(pl.multiple_of(start, 8), length)]

    swap = pltpu.make_async_remote_copy(
        src_ref=piece(buf, (1 - c) * half, half),
        dst_ref=from_twin,
        send_sem=t_sem.at[0],
        recv_sem=t_sem.at[1],
        device_id={"ch": twin},
    )
    swap.start()
    swap.wait_recv()
    acc[...] = buf[pl.ds(pl.multiple_of(c * half, 8), half), :] + from_twin[...]

    def scatter(d):
        other = lax.rem(q + d, m)
        return pltpu.make_async_remote_copy(
            src_ref=piece(acc, other * rows, rows),
            dst_ref=slots.at[d],
            send_sem=r_sem.at[0, d],
            recv_sem=r_sem.at[1, d],
            device_id={"ch": other * 2 + c},
        )

    for d in range(1, m):
        scatter(d).start()
    mine = acc[pl.ds(pl.multiple_of(q * rows, 8), rows), :]
    for d in range(1, m):
        scatter(d).wait_recv()
        mine = mine + slots[d]
    my_start = c * half + q * rows
    sums[pl.ds(pl.multiple_of(my_start, 8), rows), :] = mine

    def spread(d, start, device):
        return pltpu.make_async_remote_copy(
            src_ref=piece(sums, start, rows),
            dst_ref=piece(sums, start, rows),
            send_sem=g_sem.at[0, d],
            recv_sem=g_sem.at[1, d],
            device_id={"ch": device},
        )

    def forward(d, start):
        return pltpu.make_async_remote_copy(
            src_ref=piece(sums, start, rows),
            dst_ref=piece(sums, start, rows),
            send_sem=f_sem.at[0, d],
            recv_sem=f_sem.at[1, d],
            device_id={"ch": twin},
        )

    for d in range(1, m):
        spread(d, my_start, lax.rem(q + d, m) * 2 + c).start()
    forward(0, my_start).start()
    for d in range(1, m):
        start = c * half + lax.rem(q - d + m, m) * rows
        spread(d, start, twin).wait_recv()
        forward(d, start).start()
    for d in range(m):
        forward(d, (1 - c) * half + lax.rem(q - d + m, m) * rows).wait_recv()
    for j in range(strips):
        out_ref[:, j * 128 : (j + 1) * 128] = sums[j * height : (j + 1) * height, :]
    swap.wait_send()
    for d in range(1, m):
        scatter(d).wait_send()
        spread(d, my_start, twin).wait_send()
    for d in range(m):
        forward(d, my_start).wait_send()


def total(n, x):
    height, cols = x.shape
    area = height * (cols // 128)
    m = n // 2
    return pl.pallas_call(
        functools.partial(total_kernel, n),
        out_shape=jax.ShapeDtypeStruct(x.shape, x.dtype),
        in_specs=[pl.BlockSpec(memory_space=pltpu.VMEM)],
        out_specs=pl.BlockSpec(memory_space=pltpu.VMEM),
        scratch_shapes=[
            pltpu.VMEM((area, 128), jnp.float32),
            pltpu.VMEM((area // 2, 128), jnp.float32),
            pltpu.VMEM((area // 2, 128), jnp.float32),
            pltpu.VMEM((m, area // n, 128), jnp.float32),
            pltpu.VMEM((area, 128), jnp.float32),
            pltpu.SemaphoreType.DMA((2,)),
            pltpu.SemaphoreType.DMA((2, m)),
            pltpu.SemaphoreType.DMA((2, m)),
            pltpu.SemaphoreType.DMA((2, m)),
        ],
        compiler_params=pltpu.CompilerParams(
            collective_id=1, has_side_effects=True, vmem_limit_bytes=VMEM_LIMIT
        ),
    )(x)


def scatter_kernel(
    n, conv_ref, w_ref, p_ref, rows_ref, seen_ref, out_ref,
    g_ref, t_in, y_in, u_in, d_in, y_out, z_out, t_sem, y_sem, u_sem, d_sem, zs_sem
):
    a = n // 4
    rows = out_ref.shape[0]
    z, y, c = place(n)
    me = index_of(z, y, c)
    twin, across = index_of(z, y, 1 - c), index_of(z, 1 - y, c)
    greet([twin, across], z, a)

    def own(b):
        return pl.ds(pl.multiple_of(b * rows, rows), rows)

    def order(k):
        if k == a - 1:
            return z
        low = jnp.where(k < a - 1 - z, a - 1 - k, k - (a - 1 - z))
        high = jnp.where(k < z, k, a - 1 - (k - z))
        return jnp.where(2 * z < a, low, high)

    def to_twin(zz, side, core):
        return pltpu.make_async_remote_copy(
            src_ref=g_ref.at[own(index_of(zz, side, core))],
            dst_ref=t_in.at[zz * 2 + side],
            send_sem=t_sem.at[0, zz * 2 + side],
            recv_sem=t_sem.at[1, zz * 2 + side],
            device_id={"ch": twin},
        )

    def to_across(k, zz):
        return pltpu.make_async_remote_copy(
            src_ref=y_out.at[k],
            dst_ref=y_in.at[zz],
            send_sem=y_sem.at[0, zz],
            recv_sem=y_sem.at[1, zz],
            device_id={"ch": across},
        )

    def along(k, zz, landing, sem, device):
        return pltpu.make_async_remote_copy(
            src_ref=z_out.at[k],
            dst_ref=landing.at[zz],
            send_sem=zs_sem.at[k],
            recv_sem=sem.at[zz],
            device_id={"ch": device},
        )

    tokens = conv_ref.shape[1]
    tok_mean, inv_std = rows_ref[0:1, :], rows_ref[1:2, :]
    mean_gained, mean_both = rows_ref[2:3, :], rows_ref[3:4, :]

    def fill(zz, side, core):
        mine = own(index_of(zz, side, core))
        grad = jnp.dot(w_ref[mine, :], p_ref[...], preferred_element_type=jnp.float32)
        normed = (conv_ref[mine, :].astype(jnp.float32) - tok_mean) * inv_std
        term = (grad - mean_gained - normed * mean_both) * inv_std
        g_ref[mine, :tokens] = term.astype(jnp.bfloat16)
        g_ref[mine, tokens:] = seen_ref[mine, :]

    def cross(k):
        zz = order(k)
        to_twin(zz, 1 - y, c).wait_recv()
        y_out[k] = (
            g_ref[own(index_of(zz, 1 - y, c))].astype(jnp.float32)
            + t_in[zz * 2 + 1 - y].astype(jnp.float32)
        ).astype(jnp.bfloat16)
        to_across(k, zz).start()

    for k in range(a):
        fill(order(k), 1 - y, 1 - c)
        to_twin(order(k), 1 - y, 1 - c).start()
        fill(order(k), 1 - y, c)
        if k > 0:
            cross(k - 1)
    fill(order(0), y, 1 - c)
    to_twin(order(0), y, 1 - c).start()
    cross(a - 1)
    fill(order(0), y, c)
    for k in range(a):
        zz = order(k)
        if k < a - 1:
            fill(order(k + 1), y, 1 - c)
            to_twin(order(k + 1), y, 1 - c).start()
            fill(order(k + 1), y, c)
        to_twin(zz, y, c).wait_recv()
        to_across(k, zz).wait_recv()
        term = (
            g_ref[own(index_of(zz, y, c))].astype(jnp.float32)
            + t_in[zz * 2 + y].astype(jnp.float32)
            + y_in[zz].astype(jnp.float32)
        )
        if k < a - 1:
            out_ref[...] = term

            @pl.when((zz > z) & (z > 0))
            def _():
                along(k, zz, u_in, u_sem, me).wait_recv()
                out_ref[...] += u_in[zz].astype(jnp.float32)

            @pl.when((zz < z) & (z < a - 1))
            def _():
                along(k, zz, d_in, d_sem, me).wait_recv()
                out_ref[...] += d_in[zz].astype(jnp.float32)

            z_out[k] = out_ref[...].astype(jnp.bfloat16)

            @pl.when(zz > z)
            def _():
                along(k, zz, u_in, u_sem, me + 4).start()

            @pl.when(zz < z)
            def _():
                along(k, zz, d_in, d_sem, me - 4).start()

        else:
            out_ref[...] = term

            @pl.when(z > 0)
            def _():
                along(0, z, u_in, u_sem, me).wait_recv()
                out_ref[...] += u_in[z].astype(jnp.float32)

            @pl.when(z < a - 1)
            def _():
                along(0, z, d_in, d_sem, me).wait_recv()
                out_ref[...] += d_in[z].astype(jnp.float32)

    for k in range(a):
        zz = order(k)
        to_twin(zz, 1 - y, 1 - c).wait_send()
        to_twin(zz, y, 1 - c).wait_send()
        to_across(k, zz).wait_send()
        if k < a - 1:
            along(k, zz, u_in, u_sem, me).wait_send()


def scatter(n, conv_all, weights, pre_grad, token_rows, seen):
    rows, cols = conv_all.shape[0] // n, conv_all.shape[1] + seen.shape[1]
    a = n // 4
    return pl.pallas_call(
        functools.partial(scatter_kernel, n),
        out_shape=jax.ShapeDtypeStruct((rows, cols), jnp.float32),
        in_specs=[pl.BlockSpec(memory_space=pltpu.VMEM)] * 5,
        out_specs=pl.BlockSpec(memory_space=pltpu.VMEM),
        scratch_shapes=[
            pltpu.VMEM((n * rows, cols), jnp.bfloat16),
            pltpu.VMEM((n // 2, rows, cols), jnp.bfloat16),
            pltpu.VMEM((a, rows, cols), jnp.bfloat16),
            pltpu.VMEM((a, rows, cols), jnp.bfloat16),
            pltpu.VMEM((a, rows, cols), jnp.bfloat16),
            pltpu.VMEM((a, rows, cols), jnp.bfloat16),
            pltpu.VMEM((a, rows, cols), jnp.bfloat16),
            pltpu.SemaphoreType.DMA((2, n // 2)),
            pltpu.SemaphoreType.DMA((2, a)),
            pltpu.SemaphoreType.DMA((a,)),
            pltpu.SemaphoreType.DMA((a,)),
            pltpu.SemaphoreType.DMA((a,)),
        ],
        compiler_params=pltpu.CompilerParams(
            collective_id=2, has_side_effects=True, vmem_limit_bytes=VMEM_LIMIT
        ),
    )(conv_all, weights, pre_grad, token_rows, seen)


def dot(lhs, rhs, over, precision=None):
    return lax.dot_general(
        lhs, rhs, ((over[:1], over[1:]), ((), ())),
        precision=precision, preferred_element_type=jnp.float32,
    )


def per_device(n, features, dw_weight, norm_gain, layer_scale, w_in, w_out, w_head, labels):
    fine = lax.Precision.HIGH
    my_rows, tok_count = features.shape
    channels, class_count = w_head.shape
    row_offset = lax.axis_index("ch") * my_rows
    inputs_wide = features.astype(jnp.float32)
    classes = -(-class_count // max(n, 16)) * max(n, 16)
    head_pad = jnp.pad(w_head, ((0, 0), (0, classes - class_count)))
    scaled_head = layer_scale[:, None] * head_pad.astype(jnp.float32)
    conv_all, mixed = gather(n, features, dw_weight, w_out, scaled_head)
    conv_wide = conv_all.astype(jnp.float32)
    tok_mean = jnp.mean(conv_wide, axis=0)
    centered = conv_wide - tok_mean[None, :]
    tok_var = jnp.mean(centered * centered, axis=0)
    inv_std = 1.0 / jnp.sqrt(tok_var + norm_eps)
    norm_out = (norm_gain[:, None] * (centered * inv_std[None, :])).astype(jnp.bfloat16)
    pre_act = jnp.dot(w_in, norm_out, preferred_element_type=jnp.float32)
    gelu_out, gelu_slope = gelu_parts(pre_act)
    hidden = gelu_out.astype(jnp.bfloat16)

    my_scale = lax.dynamic_slice_in_dim(layer_scale, row_offset, my_rows, 0)
    my_head = lax.dynamic_slice_in_dim(head_pad, row_offset, my_rows, 0)
    my_head_wide = my_head.astype(jnp.float32)
    part = dot(mixed, hidden.astype(jnp.float32), (0, 0), fine) + dot(my_head, features, (0, 0))
    logits = total(n, part)

    kinds = lax.broadcasted_iota(jnp.int32, (classes, tok_count), 0)
    logits = jnp.where(kinds < class_count, logits, -jnp.inf)
    row_max = jnp.max(logits, axis=0, keepdims=True)
    exp_terms = jnp.exp(logits - row_max)
    exp_total = jnp.sum(exp_terms, axis=0, keepdims=True)
    log_total = jnp.log(exp_total) + row_max
    hit = kinds == labels[None, :]
    picked = jnp.sum(jnp.where(hit, logits, 0.0), axis=0)
    mean_loss = jnp.mean(log_total[0] - picked).reshape(1)
    logit_grad = exp_terms / exp_total - hit.astype(jnp.float32)
    grad_narrow = logit_grad.astype(jnp.bfloat16)

    out_grad = dot(my_head_wide, logit_grad, (1, 0), fine)
    seen = dot(hidden, grad_narrow, (1, 1))
    hidden_grad = dot(mixed, logit_grad, (1, 0), fine)
    seen_narrow = seen.astype(jnp.bfloat16)
    d_w_out = dot(seen_narrow, scaled_head.astype(jnp.bfloat16), (1, 1))
    branch_seen = dot(w_out, seen_narrow, (0, 0)).astype(jnp.bfloat16)
    pre_grad_wide = hidden_grad * gelu_slope
    pre_grad = pre_grad_wide.astype(jnp.bfloat16)
    d_w_in = dot(pre_grad, norm_out, (1, 1))
    gain_rows = jnp.sum(w_in.astype(jnp.float32) * norm_gain[None, :], axis=1)
    mean_gained = jnp.sum(gain_rows[:, None] * pre_grad_wide, axis=0) / channels
    mean_both = jnp.sum(pre_act * pre_grad_wide, axis=0) / channels
    weights = (w_in.astype(jnp.float32) * norm_gain[None, :]).astype(jnp.bfloat16).T
    width = -(-classes // 128) * 128
    token_rows = jnp.stack([tok_mean, inv_std, mean_gained, mean_both])
    token_rows = jnp.pad(token_rows, ((0, 4), (0, 0)))
    branch_seen = jnp.pad(branch_seen, ((0, 0), (0, width - classes)))
    landed = scatter(n, conv_all, weights, pre_grad, token_rows, branch_seen)
    conv_grad = landed[:, :tok_count]
    my_seen = landed[:, tok_count : tok_count + class_count]
    d_head = dot(inputs_wide, logit_grad, (1, 1), fine)[:, :class_count] + my_scale[:, None] * my_seen
    d_scale = jnp.sum(my_head_wide[:, :class_count] * my_seen, axis=1)
    d_features, d_dw = conv_back(conv_grad, inputs_wide, dw_weight, out_grad)
    return (d_features, d_dw, d_scale, d_w_in, d_w_out, d_head, mean_loss)


def solution(mesh):
    placed = (P("ch", "grp"), P("ch", None), P(), P(), P("ch", None), P("ch", None), P(), P("grp"))
    return jax.shard_map(
        functools.partial(per_device, mesh.shape["ch"]),
        mesh=mesh,
        in_specs=placed,
        out_specs=(
            P("ch", "grp"),
            P("ch", "grp"),
            P(("grp", "ch")),
            P(("grp", "ch"), None),
            P(("grp", "ch"), None),
            P("ch", "grp"),
            P("grp"),
        ),
        check_vma=False,
    )
```

```python
import functools
import jax
import jax.numpy as jnp
from jax import lax
from jax.experimental import pallas as pl
from jax.experimental.pallas import tpu as pltpu
from jax.sharding import PartitionSpec as P

KS = 7
WIN_H = 32
WIN_W = 32

norm_eps = 1e-06
VMEM_LIMIT = 56 * 1024 * 1024


def slide(values, rows, cols):
    area = values.shape[1]
    token = lax.broadcasted_iota(jnp.int32, values.shape, 1)
    step = rows * WIN_W + cols
    if step == 0:
        return values
    spot = (token & (WIN_W - 1)) if cols else token
    inside = (spot < (WIN_W if cols else area) - step) if step > 0 else (spot >= -step)
    return jnp.where(inside, pltpu.roll(values, (-step) % area, 1), 0.0)


def conv_rows(values, taps):
    half = KS // 2
    shifted = [slide(values, 0, j - half) for j in range(KS)]
    running = None
    for i in range(KS):
        line = sum(taps[:, i * KS + j : i * KS + j + 1] * shifted[j] for j in range(KS))
        line = slide(line, i - half, 0)
        running = line if running is None else running + line
    return running


def conv_back_kernel(grad_ref, x_ref, taps_ref, add_ref, dx_ref, dtaps_ref):
    half = KS // 2
    wide = dtaps_ref.shape[1]

    @pl.loop(0, x_ref.shape[0] // 8)
    def _(g):
        own = pl.ds(pl.multiple_of(g * 8, 8), 8)
        grad, values, taps = grad_ref[own, :], x_ref[own, :], taps_ref[own, :]
        lifted = [slide(grad, half - i, 0) for i in range(KS)]
        column = lax.broadcasted_iota(jnp.int32, (8, wide), 1)
        dtaps = jnp.zeros((8, wide), jnp.float32)
        dx = add_ref[own, :]
        for j in range(KS):
            line = sum(taps[:, i * KS + j : i * KS + j + 1] * lifted[i] for i in range(KS))
            dx = dx + slide(line, 0, half - j)
            shifted = slide(values, 0, j - half)
            for i in range(KS):
                whole = jnp.sum(lifted[i] * shifted, axis=1, keepdims=True)
                dtaps = jnp.where(column == i * KS + j, whole, dtaps)
        dx_ref[own, :] = dx
        dtaps_ref[own, :] = dtaps


def conv_back(grad, values, taps, add):
    return pl.pallas_call(
        conv_back_kernel,
        out_shape=(
            jax.ShapeDtypeStruct(grad.shape, jnp.float32),
            jax.ShapeDtypeStruct(taps.shape, jnp.float32),
        ),
        in_specs=[pl.BlockSpec(memory_space=pltpu.VMEM)] * 4,
        out_specs=(pl.BlockSpec(memory_space=pltpu.VMEM),) * 2,
        compiler_params=pltpu.CompilerParams(vmem_limit_bytes=32 * 1024 * 1024),
    )(grad, values, taps, add)


def gelu_parts(values):
    cum_prob = 0.5 * (1.0 + lax.erf(values * 0.7071067811865476))
    density = jnp.exp(-0.5 * values * values) * 0.3989422804014327
    return (values * cum_prob, cum_prob + values * density)


def place(n):
    me = lax.axis_index("ch")
    return lax.div(me, 4), lax.rem(lax.div(me, 2), 2), lax.rem(me, 2)


def index_of(z, y, c):
    return (z * 2 + y) * 2 + c


def greet(devices, z, a, between=None):
    barrier = pltpu.get_barrier_semaphore()
    for device in devices:
        pl.semaphore_signal(barrier, inc=1, device_id={"ch": device})
    me = lax.axis_index("ch")

    @pl.when(z > 0)
    def _():
        pl.semaphore_signal(barrier, inc=1, device_id={"ch": me - 4})

    @pl.when(z < a - 1)
    def _():
        pl.semaphore_signal(barrier, inc=1, device_id={"ch": me + 4})

    if between is not None:
        between()
    count = len(devices) + jnp.where(z > 0, 1, 0) + jnp.where(z < a - 1, 1, 0)
    pl.semaphore_wait(barrier, count)


def gather_kernel(
    n, x_ref, taps_ref, w_ref, head_ref, out_ref, mixed_ref, wide, conv, send_sem, recv_sem
):
    a = n // 4
    rows = x_ref.shape[0]
    parts = 2 if rows % 32 == 0 else 1
    chunk = rows // parts
    z, y, c = place(n)
    me = index_of(z, y, c)
    twin, across = index_of(z, y, 1 - c), index_of(z, 1 - y, c)

    def convolve():
        wide[...] = x_ref[...].astype(jnp.float32)

        convolve_part(0)

    def convolve_part(h):
        first = h * chunk

        @pl.loop(0, chunk // 8)
        def _(g):
            own = pl.ds(pl.multiple_of(first + g * 8, 8), 8)
            conv[own, :] = conv_rows(wide[own, :], taps_ref[own, :])

        out_ref[pl.ds(pl.multiple_of(me * rows + first, chunk), chunk)] = conv[
            first : first + chunk
        ].astype(jnp.bfloat16)

    greet([twin, across], z, a, convolve)

    def copy(kind, b, device, h):
        piece = out_ref.at[pl.ds(pl.multiple_of(b * rows + h * chunk, chunk), chunk)]
        return pltpu.make_async_remote_copy(
            src_ref=piece,
            dst_ref=piece,
            send_sem=send_sem.at[kind, b * parts + h],
            recv_sem=recv_sem.at[b * parts + h],
            device_id={"ch": device},
        )

    def send_own(h):
        @pl.when(z < a - 1)
        def _():
            copy(0, me, me + 4, h).start()

        @pl.when(z > 0)
        def _():
            copy(1, me, me - 4, h).start()

        copy(2, me, across, h).start()
        copy(3, me, twin, h).start()

    for h in range(parts):
        if h > 0:
            convolve_part(h)
        send_own(h)

    head = head_ref[...]
    high = head.astype(jnp.bfloat16)
    low = (head - high.astype(jnp.float32)).astype(jnp.bfloat16)
    units = w_ref.shape[0]
    part = min(units, 128)

    @pl.loop(0, units // part)
    def _(g):
        own = pl.ds(pl.multiple_of(g * part, part), part)
        weights = w_ref[own, :]
        mixed_ref[own, :] = jnp.dot(
            weights, high, preferred_element_type=jnp.float32
        ) + jnp.dot(weights, low, preferred_element_type=jnp.float32)

    def from_line(s, h):
        below, above = me - 4 * s, me + 4 * s

        @pl.when(z >= s)
        def _():
            copy(0, below, me, h).wait_recv()

            @pl.when(z < a - 1)
            def _():
                copy(0, below, me + 4, h).start()

            copy(2, below, across, h).start()
            copy(3, below, twin, h).start()

        @pl.when(z + s < a)
        def _():
            copy(1, above, me, h).wait_recv()

            @pl.when(z > 0)
            def _():
                copy(1, above, me - 4, h).start()

            copy(2, above, across, h).start()
            copy(3, above, twin, h).start()

    def from_across(s, h):
        def take(b):
            copy(2, b, across, h).wait_recv()
            copy(3, b, twin, h).start()

        if s == 0:
            take(across)
            return

        @pl.when(z >= s)
        def _():
            take(across - 4 * s)

        @pl.when(z + s < a)
        def _():
            take(across + 4 * s)

    for s in range(1, a):
        for h in range(parts):
            from_line(s, h)
            from_across(s - 1, h)
    for h in range(parts):
        from_across(a - 1, h)

    for h in range(parts):
        for q in range(n // 2):
            copy(3, q * 2 + 1 - c, twin, h).wait_recv()
            copy(3, q * 2 + c, twin, h).wait_send()
        for zz in range(a):
            copy(2, index_of(zz, y, c), across, h).wait_send()

            @pl.when((z < a - 1) & (zz <= z))
            def _():
                copy(0, index_of(zz, y, c), me + 4, h).wait_send()

            @pl.when((z > 0) & (zz >= z))
            def _():
                copy(1, index_of(zz, y, c), me - 4, h).wait_send()


def gather(n, x, taps, weights, head):
    rows, cols = x.shape
    return pl.pallas_call(
        functools.partial(gather_kernel, n),
        out_shape=(
            jax.ShapeDtypeStruct((n * rows, cols), x.dtype),
            jax.ShapeDtypeStruct((weights.shape[0], head.shape[1]), jnp.float32),
        ),
        in_specs=[pl.BlockSpec(memory_space=pltpu.VMEM)] * 4,
        out_specs=(pl.BlockSpec(memory_space=pltpu.VMEM),) * 2,
        scratch_shapes=[
            pltpu.VMEM((rows, cols), jnp.float32),
            pltpu.VMEM((rows, cols), jnp.float32),
            pltpu.SemaphoreType.DMA((4, 2 * n)),
            pltpu.SemaphoreType.DMA((2 * n,)),
        ],
        compiler_params=pltpu.CompilerParams(
            collective_id=0, has_side_effects=True, vmem_limit_bytes=VMEM_LIMIT
        ),
    )(x, taps, weights, head)


def total_kernel(n, x_ref, out_ref, buf, from_twin, acc, slots, sums, t_sem, r_sem, g_sem, f_sem):
    m = n // 2
    height, cols = x_ref.shape
    strips = cols // 128
    half = height * strips // 2
    rows = half // m
    me = lax.axis_index("ch")
    q, c = lax.div(me, 2), lax.rem(me, 2)
    twin = q * 2 + 1 - c
    barrier = pltpu.get_barrier_semaphore()
    pl.semaphore_signal(barrier, inc=1, device_id={"ch": twin})
    for d in range(1, m):
        pl.semaphore_signal(barrier, inc=1, device_id={"ch": lax.rem(q + d, m) * 2 + c})
    for j in range(strips):
        buf[j * height : (j + 1) * height, :] = x_ref[:, j * 128 : (j + 1) * 128]
    pl.semaphore_wait(barrier, m)

    def piece(ref, start, length):
        return ref.at[pl.ds(pl.multiple_of(start, 8), length)]

    swap = pltpu.make_async_remote_copy(
        src_ref=piece(buf, (1 - c) * half, half),
        dst_ref=from_twin,
        send_sem=t_sem.at[0],
        recv_sem=t_sem.at[1],
        device_id={"ch": twin},
    )
    swap.start()
    swap.wait_recv()
    acc[...] = buf[pl.ds(pl.multiple_of(c * half, 8), half), :] + from_twin[...]

    def scatter(d):
        other = lax.rem(q + d, m)
        return pltpu.make_async_remote_copy(
            src_ref=piece(acc, other * rows, rows),
            dst_ref=slots.at[d],
            send_sem=r_sem.at[0, d],
            recv_sem=r_sem.at[1, d],
            device_id={"ch": other * 2 + c},
        )

    for d in range(1, m):
        scatter(d).start()
    mine = acc[pl.ds(pl.multiple_of(q * rows, 8), rows), :]
    for d in range(1, m):
        scatter(d).wait_recv()
        mine = mine + slots[d]
    my_start = c * half + q * rows
    sums[pl.ds(pl.multiple_of(my_start, 8), rows), :] = mine

    def spread(d, start, device):
        return pltpu.make_async_remote_copy(
            src_ref=piece(sums, start, rows),
            dst_ref=piece(sums, start, rows),
            send_sem=g_sem.at[0, d],
            recv_sem=g_sem.at[1, d],
            device_id={"ch": device},
        )

    def forward(d, start):
        return pltpu.make_async_remote_copy(
            src_ref=piece(sums, start, rows),
            dst_ref=piece(sums, start, rows),
            send_sem=f_sem.at[0, d],
            recv_sem=f_sem.at[1, d],
            device_id={"ch": twin},
        )

    for d in range(1, m):
        spread(d, my_start, lax.rem(q + d, m) * 2 + c).start()
    forward(0, my_start).start()
    for d in range(1, m):
        start = c * half + lax.rem(q - d + m, m) * rows
        spread(d, start, twin).wait_recv()
        forward(d, start).start()
    for d in range(m):
        forward(d, (1 - c) * half + lax.rem(q - d + m, m) * rows).wait_recv()
    for j in range(strips):
        out_ref[:, j * 128 : (j + 1) * 128] = sums[j * height : (j + 1) * height, :]
    swap.wait_send()
    for d in range(1, m):
        scatter(d).wait_send()
        spread(d, my_start, twin).wait_send()
    for d in range(m):
        forward(d, my_start).wait_send()


def total(n, x):
    height, cols = x.shape
    area = height * (cols // 128)
    m = n // 2
    return pl.pallas_call(
        functools.partial(total_kernel, n),
        out_shape=jax.ShapeDtypeStruct(x.shape, x.dtype),
        in_specs=[pl.BlockSpec(memory_space=pltpu.VMEM)],
        out_specs=pl.BlockSpec(memory_space=pltpu.VMEM),
        scratch_shapes=[
            pltpu.VMEM((area, 128), jnp.float32),
            pltpu.VMEM((area // 2, 128), jnp.float32),
            pltpu.VMEM((area // 2, 128), jnp.float32),
            pltpu.VMEM((m, area // n, 128), jnp.float32),
            pltpu.VMEM((area, 128), jnp.float32),
            pltpu.SemaphoreType.DMA((2,)),
            pltpu.SemaphoreType.DMA((2, m)),
            pltpu.SemaphoreType.DMA((2, m)),
            pltpu.SemaphoreType.DMA((2, m)),
        ],
        compiler_params=pltpu.CompilerParams(
            collective_id=1, has_side_effects=True, vmem_limit_bytes=VMEM_LIMIT
        ),
    )(x)


def scatter_kernel(
    n, conv_ref, w_ref, p_ref, rows_ref, seen_ref, norm_ref, unit_ref, head_ref,
    out_ref, d_in_ref, d_out_ref,
    g_ref, t_in, y_in, u_in, d_in, y_out, z_out, t_sem, y_sem, u_sem, d_sem, zs_sem
):
    a = n // 4
    rows = out_ref.shape[0]
    z, y, c = place(n)
    me = index_of(z, y, c)
    twin, across = index_of(z, y, 1 - c), index_of(z, 1 - y, c)
    greet([twin, across], z, a)

    def own(b):
        return pl.ds(pl.multiple_of(b * rows, rows), rows)

    def order(k):
        if k == a - 1:
            return z
        low = jnp.where(k < a - 1 - z, a - 1 - k, k - (a - 1 - z))
        high = jnp.where(k < z, k, a - 1 - (k - z))
        return jnp.where(2 * z < a, low, high)

    def to_twin(zz, side, core):
        return pltpu.make_async_remote_copy(
            src_ref=g_ref.at[own(index_of(zz, side, core))],
            dst_ref=t_in.at[zz * 2 + side],
            send_sem=t_sem.at[0, zz * 2 + side],
            recv_sem=t_sem.at[1, zz * 2 + side],
            device_id={"ch": twin},
        )

    def to_across(k, zz):
        return pltpu.make_async_remote_copy(
            src_ref=y_out.at[k],
            dst_ref=y_in.at[zz],
            send_sem=y_sem.at[0, zz],
            recv_sem=y_sem.at[1, zz],
            device_id={"ch": across},
        )

    def along(k, zz, landing, sem, device):
        return pltpu.make_async_remote_copy(
            src_ref=z_out.at[k],
            dst_ref=landing.at[zz],
            send_sem=zs_sem.at[k],
            recv_sem=sem.at[zz],
            device_id={"ch": device},
        )

    tokens = conv_ref.shape[1]
    slabs = min(a, 4)
    deep = p_ref.shape[0] // slabs
    tok_mean, inv_std = rows_ref[0:1, :], rows_ref[1:2, :]
    mean_gained, mean_both = rows_ref[2:3, :], rows_ref[3:4, :]

    def fill(zz, side, core):
        mine = own(index_of(zz, side, core))
        grad = jnp.dot(w_ref[mine, :], p_ref[...], preferred_element_type=jnp.float32)
        normed = (conv_ref[mine, :].astype(jnp.float32) - tok_mean) * inv_std
        term = (grad - mean_gained - normed * mean_both) * inv_std
        g_ref[mine, :tokens] = term.astype(jnp.bfloat16)
        g_ref[mine, tokens:] = seen_ref[mine, :]

    def cross(k):
        zz = order(k)
        to_twin(zz, 1 - y, c).wait_recv()
        y_out[k] = (
            g_ref[own(index_of(zz, 1 - y, c))].astype(jnp.float32)
            + t_in[zz * 2 + 1 - y].astype(jnp.float32)
        ).astype(jnp.bfloat16)
        to_across(k, zz).start()

    for k in range(a):
        fill(order(k), 1 - y, 1 - c)
        to_twin(order(k), 1 - y, 1 - c).start()
        fill(order(k), 1 - y, c)
        if k > 0:
            cross(k - 1)
    fill(order(0), y, 1 - c)
    to_twin(order(0), y, 1 - c).start()
    cross(a - 1)
    fill(order(0), y, c)
    for k in range(a):
        zz = order(k)
        if k < a - 1:
            fill(order(k + 1), y, 1 - c)
            to_twin(order(k + 1), y, 1 - c).start()
            fill(order(k + 1), y, c)
        if k < slabs:
            slab = pl.ds(k * deep, deep)
            d_in_ref[slab, :] = dot(p_ref[slab, :], norm_ref[...], (1, 1))
            d_out_ref[slab, :] = dot(unit_ref[slab, :], head_ref[...], (1, 1))
        to_twin(zz, y, c).wait_recv()
        to_across(k, zz).wait_recv()
        term = (
            g_ref[own(index_of(zz, y, c))].astype(jnp.float32)
            + t_in[zz * 2 + y].astype(jnp.float32)
            + y_in[zz].astype(jnp.float32)
        )
        if k < a - 1:
            out_ref[...] = term

            @pl.when((zz > z) & (z > 0))
            def _():
                along(k, zz, u_in, u_sem, me).wait_recv()
                out_ref[...] += u_in[zz].astype(jnp.float32)

            @pl.when((zz < z) & (z < a - 1))
            def _():
                along(k, zz, d_in, d_sem, me).wait_recv()
                out_ref[...] += d_in[zz].astype(jnp.float32)

            z_out[k] = out_ref[...].astype(jnp.bfloat16)

            @pl.when(zz > z)
            def _():
                along(k, zz, u_in, u_sem, me + 4).start()

            @pl.when(zz < z)
            def _():
                along(k, zz, d_in, d_sem, me - 4).start()

        else:
            out_ref[...] = term

            @pl.when(z > 0)
            def _():
                along(0, z, u_in, u_sem, me).wait_recv()
                out_ref[...] += u_in[z].astype(jnp.float32)

            @pl.when(z < a - 1)
            def _():
                along(0, z, d_in, d_sem, me).wait_recv()
                out_ref[...] += d_in[z].astype(jnp.float32)

    for k in range(a):
        zz = order(k)
        to_twin(zz, 1 - y, 1 - c).wait_send()
        to_twin(zz, y, 1 - c).wait_send()
        to_across(k, zz).wait_send()
        if k < a - 1:
            along(k, zz, u_in, u_sem, me).wait_send()


def scatter(n, conv_all, weights, pre_grad, token_rows, seen, norm_out, units, head):
    rows, cols = conv_all.shape[0] // n, conv_all.shape[1] + seen.shape[1]
    a = n // 4
    return pl.pallas_call(
        functools.partial(scatter_kernel, n),
        out_shape=(
            jax.ShapeDtypeStruct((rows, cols), jnp.float32),
            jax.ShapeDtypeStruct((pre_grad.shape[0], norm_out.shape[0]), jnp.float32),
            jax.ShapeDtypeStruct((units.shape[0], head.shape[0]), jnp.float32),
        ),
        in_specs=[pl.BlockSpec(memory_space=pltpu.VMEM)] * 8,
        out_specs=(pl.BlockSpec(memory_space=pltpu.VMEM),) * 3,
        scratch_shapes=[
            pltpu.VMEM((n * rows, cols), jnp.bfloat16),
            pltpu.VMEM((n // 2, rows, cols), jnp.bfloat16),
            pltpu.VMEM((a, rows, cols), jnp.bfloat16),
            pltpu.VMEM((a, rows, cols), jnp.bfloat16),
            pltpu.VMEM((a, rows, cols), jnp.bfloat16),
            pltpu.VMEM((a, rows, cols), jnp.bfloat16),
            pltpu.VMEM((a, rows, cols), jnp.bfloat16),
            pltpu.SemaphoreType.DMA((2, n // 2)),
            pltpu.SemaphoreType.DMA((2, a)),
            pltpu.SemaphoreType.DMA((a,)),
            pltpu.SemaphoreType.DMA((a,)),
            pltpu.SemaphoreType.DMA((a,)),
        ],
        compiler_params=pltpu.CompilerParams(
            collective_id=2, has_side_effects=True, vmem_limit_bytes=VMEM_LIMIT
        ),
    )(conv_all, weights, pre_grad, token_rows, seen, norm_out, units, head)


def dot(lhs, rhs, over, precision=None):
    return lax.dot_general(
        lhs, rhs, ((over[:1], over[1:]), ((), ())),
        precision=precision, preferred_element_type=jnp.float32,
    )


def per_device(n, features, dw_weight, norm_gain, layer_scale, w_in, w_out, w_head, labels):
    fine = lax.Precision.HIGH
    my_rows, tok_count = features.shape
    channels, class_count = w_head.shape
    row_offset = lax.axis_index("ch") * my_rows
    inputs_wide = features.astype(jnp.float32)
    classes = -(-class_count // max(n, 16)) * max(n, 16)
    head_pad = jnp.pad(w_head, ((0, 0), (0, classes - class_count)))
    scaled_head = layer_scale[:, None] * head_pad.astype(jnp.float32)
    conv_all, mixed = gather(n, features, dw_weight, w_out, scaled_head)
    conv_wide = conv_all.astype(jnp.float32)
    tok_mean = jnp.mean(conv_wide, axis=0)
    centered = conv_wide - tok_mean[None, :]
    tok_var = jnp.mean(centered * centered, axis=0)
    inv_std = 1.0 / jnp.sqrt(tok_var + norm_eps)
    norm_out = (norm_gain[:, None] * (centered * inv_std[None, :])).astype(jnp.bfloat16)
    pre_act = jnp.dot(w_in, norm_out, preferred_element_type=jnp.float32)
    gelu_out, gelu_slope = gelu_parts(pre_act)
    hidden = gelu_out.astype(jnp.bfloat16)

    my_scale = lax.dynamic_slice_in_dim(layer_scale, row_offset, my_rows, 0)
    my_head = lax.dynamic_slice_in_dim(head_pad, row_offset, my_rows, 0)
    my_head_wide = my_head.astype(jnp.float32)
    part = dot(mixed, hidden.astype(jnp.float32), (0, 0), fine) + dot(my_head, features, (0, 0))
    logits = total(n, part)

    kinds = lax.broadcasted_iota(jnp.int32, (classes, tok_count), 0)
    logits = jnp.where(kinds < class_count, logits, -jnp.inf)
    row_max = jnp.max(logits, axis=0, keepdims=True)
    exp_terms = jnp.exp(logits - row_max)
    exp_total = jnp.sum(exp_terms, axis=0, keepdims=True)
    log_total = jnp.log(exp_total) + row_max
    hit = kinds == labels[None, :]
    picked = jnp.sum(jnp.where(hit, logits, 0.0), axis=0)
    mean_loss = jnp.mean(log_total[0] - picked).reshape(1)
    logit_grad = exp_terms / exp_total - hit.astype(jnp.float32)
    grad_narrow = logit_grad.astype(jnp.bfloat16)

    out_grad = dot(my_head_wide, logit_grad, (1, 0), fine)
    seen = dot(hidden, grad_narrow, (1, 1))
    hidden_grad = dot(mixed, logit_grad, (1, 0), fine)
    seen_narrow = seen.astype(jnp.bfloat16)
    branch_seen = dot(w_out, seen_narrow, (0, 0)).astype(jnp.bfloat16)
    pre_grad_wide = hidden_grad * gelu_slope
    pre_grad = pre_grad_wide.astype(jnp.bfloat16)
    gain_rows = jnp.sum(w_in.astype(jnp.float32) * norm_gain[None, :], axis=1)
    mean_gained = jnp.sum(gain_rows[:, None] * pre_grad_wide, axis=0) / channels
    mean_both = jnp.sum(pre_act * pre_grad_wide, axis=0) / channels
    weights = (w_in.astype(jnp.float32) * norm_gain[None, :]).astype(jnp.bfloat16).T
    width = -(-classes // 128) * 128
    token_rows = jnp.stack([tok_mean, inv_std, mean_gained, mean_both])
    token_rows = jnp.pad(token_rows, ((0, 4), (0, 0)))
    branch_seen = jnp.pad(branch_seen, ((0, 0), (0, width - classes)))
    landed, d_w_in, d_w_out = scatter(
        n, conv_all, weights, pre_grad, token_rows, branch_seen,
        norm_out, seen_narrow, scaled_head.astype(jnp.bfloat16),
    )
    conv_grad = landed[:, :tok_count]
    my_seen = landed[:, tok_count : tok_count + class_count]
    d_head = dot(inputs_wide, logit_grad, (1, 1), fine)[:, :class_count] + my_scale[:, None] * my_seen
    d_scale = jnp.sum(my_head_wide[:, :class_count] * my_seen, axis=1)
    d_features, d_dw = conv_back(conv_grad, inputs_wide, dw_weight, out_grad)
    return (d_features, d_dw, d_scale, d_w_in, d_w_out, d_head, mean_loss)


def solution(mesh):
    placed = (P("ch", "grp"), P("ch", None), P(), P(), P("ch", None), P("ch", None), P(), P("grp"))
    return jax.shard_map(
        functools.partial(per_device, mesh.shape["ch"]),
        mesh=mesh,
        in_specs=placed,
        out_specs=(
            P("ch", "grp"),
            P("ch", "grp"),
            P(("grp", "ch")),
            P(("grp", "ch"), None),
            P(("grp", "ch"), None),
            P("ch", "grp"),
            P("grp"),
        ),
        check_vma=False,
    )
```

```python
import functools
import jax
import jax.numpy as jnp
from jax import lax
from jax.experimental import pallas as pl
from jax.experimental.pallas import tpu as pltpu
from jax.sharding import PartitionSpec as P

KS = 7
WIN_H = 32
WIN_W = 32

norm_eps = 1e-06
VMEM_LIMIT = 56 * 1024 * 1024


def slide(values, rows, cols):
    area = values.shape[1]
    token = lax.broadcasted_iota(jnp.int32, values.shape, 1)
    step = rows * WIN_W + cols
    if step == 0:
        return values
    spot = (token & (WIN_W - 1)) if cols else token
    inside = (spot < (WIN_W if cols else area) - step) if step > 0 else (spot >= -step)
    return jnp.where(inside, pltpu.roll(values, (-step) % area, 1), 0.0)


def conv_rows(values, taps):
    half = KS // 2
    shifted = [slide(values, 0, j - half) for j in range(KS)]
    running = None
    for i in range(KS):
        line = sum(taps[:, i * KS + j : i * KS + j + 1] * shifted[j] for j in range(KS))
        line = slide(line, i - half, 0)
        running = line if running is None else running + line
    return running


def conv_back_kernel(grad_ref, x_ref, taps_ref, add_ref, dx_ref, dtaps_ref):
    half = KS // 2
    wide = dtaps_ref.shape[1]

    @pl.loop(0, x_ref.shape[0] // 8)
    def _(g):
        own = pl.ds(pl.multiple_of(g * 8, 8), 8)
        grad, values, taps = grad_ref[own, :], x_ref[own, :], taps_ref[own, :]
        lifted = [slide(grad, half - i, 0) for i in range(KS)]
        column = lax.broadcasted_iota(jnp.int32, (8, wide), 1)
        dtaps = jnp.zeros((8, wide), jnp.float32)
        dx = add_ref[own, :]
        for j in range(KS):
            line = sum(taps[:, i * KS + j : i * KS + j + 1] * lifted[i] for i in range(KS))
            dx = dx + slide(line, 0, half - j)
            shifted = slide(values, 0, j - half)
            for i in range(KS):
                whole = jnp.sum(lifted[i] * shifted, axis=1, keepdims=True)
                dtaps = jnp.where(column == i * KS + j, whole, dtaps)
        dx_ref[own, :] = dx
        dtaps_ref[own, :] = dtaps


def conv_back(grad, values, taps, add):
    return pl.pallas_call(
        conv_back_kernel,
        out_shape=(
            jax.ShapeDtypeStruct(grad.shape, jnp.float32),
            jax.ShapeDtypeStruct(taps.shape, jnp.float32),
        ),
        in_specs=[pl.BlockSpec(memory_space=pltpu.VMEM)] * 4,
        out_specs=(pl.BlockSpec(memory_space=pltpu.VMEM),) * 2,
        compiler_params=pltpu.CompilerParams(vmem_limit_bytes=32 * 1024 * 1024),
    )(grad, values, taps, add)


def gelu_parts(values):
    cum_prob = 0.5 * (1.0 + lax.erf(values * 0.7071067811865476))
    density = jnp.exp(-0.5 * values * values) * 0.3989422804014327
    return (values * cum_prob, cum_prob + values * density)


def place(n):
    me = lax.axis_index("ch")
    return lax.div(me, 4), lax.rem(lax.div(me, 2), 2), lax.rem(me, 2)


def index_of(z, y, c):
    return (z * 2 + y) * 2 + c


def greet(devices, z, a, between=None):
    barrier = pltpu.get_barrier_semaphore()
    for device in devices:
        pl.semaphore_signal(barrier, inc=1, device_id={"ch": device})
    me = lax.axis_index("ch")

    @pl.when(z > 0)
    def _():
        pl.semaphore_signal(barrier, inc=1, device_id={"ch": me - 4})

    @pl.when(z < a - 1)
    def _():
        pl.semaphore_signal(barrier, inc=1, device_id={"ch": me + 4})

    if between is not None:
        between()
    count = len(devices) + jnp.where(z > 0, 1, 0) + jnp.where(z < a - 1, 1, 0)
    pl.semaphore_wait(barrier, count)


def gather_kernel(
    n, x_ref, taps_ref, w_ref, head_ref, out_ref, mixed_ref, wide, conv, send_sem, recv_sem
):
    a = n // 4
    rows = x_ref.shape[0]
    parts = 2 if rows % 32 == 0 else 1
    chunk = rows // parts
    z, y, c = place(n)
    me = index_of(z, y, c)
    twin, across = index_of(z, y, 1 - c), index_of(z, 1 - y, c)

    def convolve():
        wide[...] = x_ref[...].astype(jnp.float32)

        convolve_part(0)

    def convolve_part(h):
        first = h * chunk

        @pl.loop(0, chunk // 8)
        def _(g):
            own = pl.ds(pl.multiple_of(first + g * 8, 8), 8)
            conv[own, :] = conv_rows(wide[own, :], taps_ref[own, :])

        out_ref[pl.ds(pl.multiple_of(me * rows + first, chunk), chunk)] = conv[
            first : first + chunk
        ].astype(jnp.bfloat16)

    greet([twin, across], z, a, convolve)

    def copy(kind, b, device, h):
        piece = out_ref.at[pl.ds(pl.multiple_of(b * rows + h * chunk, chunk), chunk)]
        return pltpu.make_async_remote_copy(
            src_ref=piece,
            dst_ref=piece,
            send_sem=send_sem.at[kind, b * parts + h],
            recv_sem=recv_sem.at[b * parts + h],
            device_id={"ch": device},
        )

    def send_own(h):
        @pl.when(z < a - 1)
        def _():
            copy(0, me, me + 4, h).start()

        @pl.when(z > 0)
        def _():
            copy(1, me, me - 4, h).start()

        copy(2, me, across, h).start()
        copy(3, me, twin, h).start()

    for h in range(parts):
        if h > 0:
            convolve_part(h)
        send_own(h)

    head = head_ref[...]
    high = head.astype(jnp.bfloat16)
    low = (head - high.astype(jnp.float32)).astype(jnp.bfloat16)
    units = w_ref.shape[0]
    part = min(units, 128)

    @pl.loop(0, units // part)
    def _(g):
        own = pl.ds(pl.multiple_of(g * part, part), part)
        weights = w_ref[own, :]
        mixed_ref[own, :] = jnp.dot(
            weights, high, preferred_element_type=jnp.float32
        ) + jnp.dot(weights, low, preferred_element_type=jnp.float32)

    def from_line(s, h):
        below, above = me - 4 * s, me + 4 * s

        @pl.when(z >= s)
        def _():
            copy(0, below, me, h).wait_recv()

            @pl.when(z < a - 1)
            def _():
                copy(0, below, me + 4, h).start()

            copy(2, below, across, h).start()
            copy(3, below, twin, h).start()

        @pl.when(z + s < a)
        def _():
            copy(1, above, me, h).wait_recv()

            @pl.when(z > 0)
            def _():
                copy(1, above, me - 4, h).start()

            copy(2, above, across, h).start()
            copy(3, above, twin, h).start()

    def from_across(s, h):
        def take(b):
            copy(2, b, across, h).wait_recv()
            copy(3, b, twin, h).start()

        if s == 0:
            take(across)
            return

        @pl.when(z >= s)
        def _():
            take(across - 4 * s)

        @pl.when(z + s < a)
        def _():
            take(across + 4 * s)

    for s in range(1, a):
        for h in range(parts):
            from_line(s, h)
            from_across(s - 1, h)
    for h in range(parts):
        from_across(a - 1, h)

    for h in range(parts):
        for q in range(n // 2):
            copy(3, q * 2 + 1 - c, twin, h).wait_recv()
            copy(3, q * 2 + c, twin, h).wait_send()
        for zz in range(a):
            copy(2, index_of(zz, y, c), across, h).wait_send()

            @pl.when((z < a - 1) & (zz <= z))
            def _():
                copy(0, index_of(zz, y, c), me + 4, h).wait_send()

            @pl.when((z > 0) & (zz >= z))
            def _():
                copy(1, index_of(zz, y, c), me - 4, h).wait_send()


def gather(n, x, taps, weights, head):
    rows, cols = x.shape
    return pl.pallas_call(
        functools.partial(gather_kernel, n),
        out_shape=(
            jax.ShapeDtypeStruct((n * rows, cols), x.dtype),
            jax.ShapeDtypeStruct((weights.shape[0], head.shape[1]), jnp.float32),
        ),
        in_specs=[pl.BlockSpec(memory_space=pltpu.VMEM)] * 4,
        out_specs=(pl.BlockSpec(memory_space=pltpu.VMEM),) * 2,
        scratch_shapes=[
            pltpu.VMEM((rows, cols), jnp.float32),
            pltpu.VMEM((rows, cols), jnp.float32),
            pltpu.SemaphoreType.DMA((4, 2 * n)),
            pltpu.SemaphoreType.DMA((2 * n,)),
        ],
        compiler_params=pltpu.CompilerParams(
            collective_id=0, has_side_effects=True, vmem_limit_bytes=VMEM_LIMIT
        ),
    )(x, taps, weights, head)


def total_kernel(n, x_ref, out_ref, buf, from_twin, acc, slots, sums, t_sem, r_sem, g_sem, f_sem):
    m = n // 2
    height, cols = x_ref.shape
    strips = cols // 128
    half = height * strips // 2
    rows = half // m
    me = lax.axis_index("ch")
    q, c = lax.div(me, 2), lax.rem(me, 2)
    twin = q * 2 + 1 - c
    barrier = pltpu.get_barrier_semaphore()
    pl.semaphore_signal(barrier, inc=1, device_id={"ch": twin})
    for d in range(1, m):
        pl.semaphore_signal(barrier, inc=1, device_id={"ch": lax.rem(q + d, m) * 2 + c})
    for j in range(strips):
        buf[j * height : (j + 1) * height, :] = x_ref[:, j * 128 : (j + 1) * 128]
    pl.semaphore_wait(barrier, m)

    def piece(ref, start, length):
        return ref.at[pl.ds(pl.multiple_of(start, 8), length)]

    swap = pltpu.make_async_remote_copy(
        src_ref=piece(buf, (1 - c) * half, half),
        dst_ref=from_twin,
        send_sem=t_sem.at[0],
        recv_sem=t_sem.at[1],
        device_id={"ch": twin},
    )
    swap.start()
    swap.wait_recv()
    acc[...] = buf[pl.ds(pl.multiple_of(c * half, 8), half), :] + from_twin[...]

    def scatter(d):
        other = lax.rem(q + d, m)
        return pltpu.make_async_remote_copy(
            src_ref=piece(acc, other * rows, rows),
            dst_ref=slots.at[d],
            send_sem=r_sem.at[0, d],
            recv_sem=r_sem.at[1, d],
            device_id={"ch": other * 2 + c},
        )

    for d in range(1, m):
        scatter(d).start()
    mine = acc[pl.ds(pl.multiple_of(q * rows, 8), rows), :]
    for d in range(1, m):
        scatter(d).wait_recv()
        mine = mine + slots[d]
    my_start = c * half + q * rows
    sums[pl.ds(pl.multiple_of(my_start, 8), rows), :] = mine

    def spread(d, start, device):
        return pltpu.make_async_remote_copy(
            src_ref=piece(sums, start, rows),
            dst_ref=piece(sums, start, rows),
            send_sem=g_sem.at[0, d],
            recv_sem=g_sem.at[1, d],
            device_id={"ch": device},
        )

    def forward(d, start):
        return pltpu.make_async_remote_copy(
            src_ref=piece(sums, start, rows),
            dst_ref=piece(sums, start, rows),
            send_sem=f_sem.at[0, d],
            recv_sem=f_sem.at[1, d],
            device_id={"ch": twin},
        )

    for d in range(1, m):
        spread(d, my_start, lax.rem(q + d, m) * 2 + c).start()
    forward(0, my_start).start()
    for d in range(1, m):
        start = c * half + lax.rem(q - d + m, m) * rows
        spread(d, start, twin).wait_recv()
        forward(d, start).start()
    for d in range(m):
        forward(d, (1 - c) * half + lax.rem(q - d + m, m) * rows).wait_recv()
    for j in range(strips):
        out_ref[:, j * 128 : (j + 1) * 128] = sums[j * height : (j + 1) * height, :]
    swap.wait_send()
    for d in range(1, m):
        scatter(d).wait_send()
        spread(d, my_start, twin).wait_send()
    for d in range(m):
        forward(d, my_start).wait_send()


def total(n, x):
    height, cols = x.shape
    area = height * (cols // 128)
    m = n // 2
    return pl.pallas_call(
        functools.partial(total_kernel, n),
        out_shape=jax.ShapeDtypeStruct(x.shape, x.dtype),
        in_specs=[pl.BlockSpec(memory_space=pltpu.VMEM)],
        out_specs=pl.BlockSpec(memory_space=pltpu.VMEM),
        scratch_shapes=[
            pltpu.VMEM((area, 128), jnp.float32),
            pltpu.VMEM((area // 2, 128), jnp.float32),
            pltpu.VMEM((area // 2, 128), jnp.float32),
            pltpu.VMEM((m, area // n, 128), jnp.float32),
            pltpu.VMEM((area, 128), jnp.float32),
            pltpu.SemaphoreType.DMA((2,)),
            pltpu.SemaphoreType.DMA((2, m)),
            pltpu.SemaphoreType.DMA((2, m)),
            pltpu.SemaphoreType.DMA((2, m)),
        ],
        compiler_params=pltpu.CompilerParams(
            collective_id=1, has_side_effects=True, vmem_limit_bytes=VMEM_LIMIT
        ),
    )(x)


def scatter_kernel(
    n, conv_ref, w_ref, p_ref, rows_ref, seen_ref, out_ref,
    g_ref, t_in, y_in, u_in, d_in, y_out, z_out, t_sem, y_sem, u_sem, d_sem, zs_sem
):
    a = n // 4
    rows = out_ref.shape[0]
    z, y, c = place(n)
    me = index_of(z, y, c)
    twin, across = index_of(z, y, 1 - c), index_of(z, 1 - y, c)
    greet([twin, across], z, a)

    def own(b):
        return pl.ds(pl.multiple_of(b * rows, rows), rows)

    def order(k):
        if k == a - 1:
            return z
        low = jnp.where(k < a - 1 - z, a - 1 - k, k - (a - 1 - z))
        high = jnp.where(k < z, k, a - 1 - (k - z))
        return jnp.where(2 * z < a, low, high)

    def to_twin(zz, side, core):
        return pltpu.make_async_remote_copy(
            src_ref=g_ref.at[own(index_of(zz, side, core))],
            dst_ref=t_in.at[zz * 2 + side],
            send_sem=t_sem.at[0, zz * 2 + side],
            recv_sem=t_sem.at[1, zz * 2 + side],
            device_id={"ch": twin},
        )

    def to_across(k, zz):
        return pltpu.make_async_remote_copy(
            src_ref=y_out.at[k],
            dst_ref=y_in.at[zz],
            send_sem=y_sem.at[0, zz],
            recv_sem=y_sem.at[1, zz],
            device_id={"ch": across},
        )

    def along(k, zz, landing, sem, device):
        return pltpu.make_async_remote_copy(
            src_ref=z_out.at[k],
            dst_ref=landing.at[zz],
            send_sem=zs_sem.at[k],
            recv_sem=sem.at[zz],
            device_id={"ch": device},
        )

    tokens = conv_ref.shape[1]
    tok_mean, inv_std = rows_ref[0:1, :], rows_ref[1:2, :]
    mean_gained, mean_both = rows_ref[2:3, :], rows_ref[3:4, :]

    def fill(zz, side, core):
        mine = own(index_of(zz, side, core))
        grad = jnp.dot(w_ref[mine, :], p_ref[...], preferred_element_type=jnp.float32)
        normed = (conv_ref[mine, :].astype(jnp.float32) - tok_mean) * inv_std
        term = (grad - mean_gained - normed * mean_both) * inv_std
        g_ref[mine, :tokens] = term.astype(jnp.bfloat16)
        g_ref[mine, tokens:] = seen_ref[mine, :]

    def cross(k):
        zz = order(k)
        to_twin(zz, 1 - y, c).wait_recv()
        y_out[k] = (
            g_ref[own(index_of(zz, 1 - y, c))].astype(jnp.float32)
            + t_in[zz * 2 + 1 - y].astype(jnp.float32)
        ).astype(jnp.bfloat16)
        to_across(k, zz).start()

    for k in range(a):
        fill(order(k), 1 - y, 1 - c)
        to_twin(order(k), 1 - y, 1 - c).start()
        fill(order(k), 1 - y, c)
        if k > 0:
            cross(k - 1)
    fill(order(0), y, 1 - c)
    to_twin(order(0), y, 1 - c).start()
    cross(a - 1)
    fill(order(0), y, c)
    for k in range(a):
        zz = order(k)
        if k < a - 1:
            fill(order(k + 1), y, 1 - c)
            to_twin(order(k + 1), y, 1 - c).start()
            fill(order(k + 1), y, c)
        to_twin(zz, y, c).wait_recv()
        to_across(k, zz).wait_recv()
        term = (
            g_ref[own(index_of(zz, y, c))].astype(jnp.float32)
            + t_in[zz * 2 + y].astype(jnp.float32)
            + y_in[zz].astype(jnp.float32)
        )
        if k < a - 1:
            out_ref[...] = term

            @pl.when((zz > z) & (z > 0))
            def _():
                along(k, zz, u_in, u_sem, me).wait_recv()
                out_ref[...] += u_in[zz].astype(jnp.float32)

            @pl.when((zz < z) & (z < a - 1))
            def _():
                along(k, zz, d_in, d_sem, me).wait_recv()
                out_ref[...] += d_in[zz].astype(jnp.float32)

            z_out[k] = out_ref[...].astype(jnp.bfloat16)

            @pl.when(zz > z)
            def _():
                along(k, zz, u_in, u_sem, me + 4).start()

            @pl.when(zz < z)
            def _():
                along(k, zz, d_in, d_sem, me - 4).start()

        else:
            out_ref[...] = term

            @pl.when(z > 0)
            def _():
                along(0, z, u_in, u_sem, me).wait_recv()
                out_ref[...] += u_in[z].astype(jnp.float32)

            @pl.when(z < a - 1)
            def _():
                along(0, z, d_in, d_sem, me).wait_recv()
                out_ref[...] += d_in[z].astype(jnp.float32)

    for k in range(a):
        zz = order(k)
        to_twin(zz, 1 - y, 1 - c).wait_send()
        to_twin(zz, y, 1 - c).wait_send()
        to_across(k, zz).wait_send()
        if k < a - 1:
            along(k, zz, u_in, u_sem, me).wait_send()


def scatter(n, conv_all, weights, pre_grad, token_rows, seen):
    rows, cols = conv_all.shape[0] // n, conv_all.shape[1] + seen.shape[1]
    a = n // 4
    return pl.pallas_call(
        functools.partial(scatter_kernel, n),
        out_shape=jax.ShapeDtypeStruct((rows, cols), jnp.float32),
        in_specs=[pl.BlockSpec(memory_space=pltpu.VMEM)] * 5,
        out_specs=pl.BlockSpec(memory_space=pltpu.VMEM),
        scratch_shapes=[
            pltpu.VMEM((n * rows, cols), jnp.bfloat16),
            pltpu.VMEM((n // 2, rows, cols), jnp.bfloat16),
            pltpu.VMEM((a, rows, cols), jnp.bfloat16),
            pltpu.VMEM((a, rows, cols), jnp.bfloat16),
            pltpu.VMEM((a, rows, cols), jnp.bfloat16),
            pltpu.VMEM((a, rows, cols), jnp.bfloat16),
            pltpu.VMEM((a, rows, cols), jnp.bfloat16),
            pltpu.SemaphoreType.DMA((2, n // 2)),
            pltpu.SemaphoreType.DMA((2, a)),
            pltpu.SemaphoreType.DMA((a,)),
            pltpu.SemaphoreType.DMA((a,)),
            pltpu.SemaphoreType.DMA((a,)),
        ],
        compiler_params=pltpu.CompilerParams(
            collective_id=2, has_side_effects=True, vmem_limit_bytes=VMEM_LIMIT
        ),
    )(conv_all, weights, pre_grad, token_rows, seen)


def dot(lhs, rhs, over, precision=None):
    return lax.dot_general(
        lhs, rhs, ((over[:1], over[1:]), ((), ())),
        precision=precision, preferred_element_type=jnp.float32,
    )


def per_device(n, features, dw_weight, norm_gain, layer_scale, w_in, w_out, w_head, labels):
    fine = lax.Precision.HIGH
    my_rows, tok_count = features.shape
    channels, class_count = w_head.shape
    row_offset = lax.axis_index("ch") * my_rows
    inputs_wide = features.astype(jnp.float32)
    classes = -(-class_count // max(n, 16)) * max(n, 16)
    head_pad = jnp.pad(w_head, ((0, 0), (0, classes - class_count)))
    scaled_head = layer_scale[:, None] * head_pad.astype(jnp.float32)
    conv_all, mixed = gather(n, features, dw_weight, w_out, scaled_head)
    conv_wide = conv_all.astype(jnp.float32)
    tok_mean = jnp.mean(conv_wide, axis=0)
    centered = conv_wide - tok_mean[None, :]
    tok_var = jnp.mean(centered * centered, axis=0)
    inv_std = 1.0 / jnp.sqrt(tok_var + norm_eps)
    norm_out = (norm_gain[:, None] * (centered * inv_std[None, :])).astype(jnp.bfloat16)
    pre_act = jnp.dot(w_in, norm_out, preferred_element_type=jnp.float32)
    gelu_out, gelu_slope = gelu_parts(pre_act)
    hidden = gelu_out.astype(jnp.bfloat16)

    my_scale = lax.dynamic_slice_in_dim(layer_scale, row_offset, my_rows, 0)
    my_head = lax.dynamic_slice_in_dim(head_pad, row_offset, my_rows, 0)
    my_head_wide = my_head.astype(jnp.float32)
    part = dot(mixed, hidden.astype(jnp.float32), (0, 0), fine) + dot(my_head, features, (0, 0))
    logits = total(n, part)

    kinds = lax.broadcasted_iota(jnp.int32, (classes, tok_count), 0)
    logits = jnp.where(kinds < class_count, logits, -jnp.inf)
    row_max = jnp.max(logits, axis=0, keepdims=True)
    exp_terms = jnp.exp(logits - row_max)
    exp_total = jnp.sum(exp_terms, axis=0, keepdims=True)
    log_total = jnp.log(exp_total) + row_max
    hit = kinds == labels[None, :]
    picked = jnp.sum(jnp.where(hit, logits, 0.0), axis=0)
    mean_loss = jnp.mean(log_total[0] - picked).reshape(1)
    logit_grad = exp_terms / exp_total - hit.astype(jnp.float32)
    grad_narrow = logit_grad.astype(jnp.bfloat16)

    out_grad = dot(my_head_wide, logit_grad, (1, 0), fine)
    seen = dot(hidden, grad_narrow, (1, 1))
    hidden_grad = dot(mixed, logit_grad, (1, 0), fine)
    seen_narrow = seen.astype(jnp.bfloat16)
    d_w_out = dot(seen_narrow, scaled_head.astype(jnp.bfloat16), (1, 1))
    branch_seen = dot(w_out, seen_narrow, (0, 0)).astype(jnp.bfloat16)
    pre_grad_wide = hidden_grad * gelu_slope
    pre_grad = pre_grad_wide.astype(jnp.bfloat16)
    d_w_in = dot(pre_grad, norm_out, (1, 1))
    gain_rows = jnp.sum(w_in.astype(jnp.float32) * norm_gain[None, :], axis=1)
    mean_gained = jnp.sum(gain_rows[:, None] * pre_grad_wide, axis=0) / channels
    mean_both = jnp.sum(pre_act * pre_grad_wide, axis=0) / channels
    weights = (w_in.astype(jnp.float32) * norm_gain[None, :]).astype(jnp.bfloat16).T
    width = -(-classes // 128) * 128
    token_rows = jnp.stack([tok_mean, inv_std, mean_gained, mean_both])
    token_rows = jnp.pad(token_rows, ((0, 4), (0, 0)))
    branch_seen = jnp.pad(branch_seen, ((0, 0), (0, width - classes)))
    landed = scatter(n, conv_all, weights, pre_grad, token_rows, branch_seen)
    conv_grad = landed[:, :tok_count]
    my_seen = landed[:, tok_count : tok_count + class_count]
    d_head = dot(inputs_wide, logit_grad, (1, 1), fine)[:, :class_count] + my_scale[:, None] * my_seen
    d_scale = jnp.sum(my_head_wide[:, :class_count] * my_seen, axis=1)
    d_features, d_dw = conv_back(conv_grad, inputs_wide, dw_weight, out_grad)
    return (d_features, d_dw, d_scale, d_w_in, d_w_out, d_head, mean_loss)


def solution(mesh):
    placed = (P("ch", "grp"), P("ch", None), P(), P(), P("ch", None), P("ch", None), P(), P("grp"))
    return jax.shard_map(
        functools.partial(per_device, mesh.shape["ch"]),
        mesh=mesh,
        in_specs=placed,
        out_specs=(
            P("ch", "grp"),
            P("ch", "grp"),
            P(("grp", "ch")),
            P(("grp", "ch"), None),
            P(("grp", "ch"), None),
            P("ch", "grp"),
            P("grp"),
        ),
        check_vma=False,
    )
```
